256 devices in a mesh: heads: 4 (over y_lo, core), tokens: 64 (over x, z, y_hi).
Axes of the slice: x: 4, y: 4 (y_hi: 2, y_lo: 2; y = y_hi * 2 + y_lo), z: 8, core: 2. Of those that a mesh axis runs over, the one named last changes fastest.
Arguments:
- queries: bfloat16 [32768, 4096], P(('heads', 'tokens')), may hold values from -6 to 6
- keys: bfloat16 [32768, 4096], P(('heads', 'tokens')), may hold values from -6 to 6
- values: bfloat16 [32768, 4096], P(('heads', 'tokens')), may hold values from -6 to 6
- rates: float32 [32768, 8], P(('heads', 'tokens')), may hold values from 0.0003 to 0.003
- gate_fast: bfloat16 [8, 512, 512], P('heads'), may hold values from -0.25 to 0.25
- down_fast: bfloat16 [8, 512, 512], P('heads'), may hold values from -0.25 to 0.25
- up_fast: bfloat16 [8, 512, 512], P('heads'), may hold values from -0.25 to 0.25
Outputs:
- outputs: bfloat16 [32768, 4096], P(('heads', 'tokens'))
- gate_next: bfloat16 [8, 512, 512], P('heads')
- down_next: bfloat16 [8, 512, 512], P('heads')
- up_next: bfloat16 [8, 512, 512], P('heads')
The draws below stay inside these ranges and needn't reach their ends.
All inputs are finite; a program needn't handle non-finite values.
Results may differ from the reference program's by a relative error of at most 0.025.
Values may be sent and summed in bfloat16 or wider, within the bound.
A program may use at most 64 MiB of HBM per device.

```python
import math
import jax
import jax.numpy as jnp
from jax import lax

H = 8
DH = 512
D = 4096
TOKENS = 32768


def shard_levels(key, extent, pieces, low, high):
    def one(dim, blocks):
        steps = jax.random.uniform(jax.random.fold_in(jax.random.fold_in(key, 6), dim), (blocks,), jnp.float32, low / len(pieces), high / len(pieces))
        return jnp.repeat(jnp.exp(steps), extent[dim] // blocks).reshape((-1,) + (1,) * (len(extent) - dim - 1))

    level = one(*pieces[0])
    for cut in pieces[1:]:
        level = level * one(*cut)
    return level


def bell_draw(own_key, shape, width, limit, split=(), dtype=jnp.bfloat16):
    entries = width * jax.random.normal(own_key, shape, jnp.float32)
    if split:
        entries = entries * shard_levels(own_key, shape, split, -0.22, 0.18)
    return jnp.clip(entries, -limit, limit).astype(dtype)


def setup_inputs(seed: int = 0) -> dict:
    key_of = jax.random.split(jax.random.key(seed), 8)
    return {
        "queries": bell_draw(key_of[0], (TOKENS, D), 1.0, 6.0, ((0, 256),)),
        "keys": bell_draw(key_of[1], (TOKENS, D), 1.0, 6.0, ((0, 256),)),
        "values": bell_draw(key_of[2], (TOKENS, D), 1.0, 6.0, ((0, 256),)),
        "rates": jnp.clip(jnp.exp(math.log(0.003) - 2.3025851 * jax.random.uniform(key_of[3], (TOKENS, H), jnp.float32) ** shard_levels(key_of[3], (TOKENS, H), ((0, 256),), -0.2, 0.2)), 0.0003, 0.003),
        "gate_fast": bell_draw(key_of[4], (H, DH, DH), DH ** -0.5, 0.25, ((0, 4),)),
        "down_fast": bell_draw(key_of[5], (H, DH, DH), DH ** -0.5, 0.25, ((0, 4),)),
        "up_fast": bell_draw(key_of[6], (H, DH, DH), DH ** -0.5, 0.25, ((0, 4),)),
    }


def inner_sum(left, right):
    return lax.dot_general(left, right, (((0,), (0,)), ((), ())), preferred_element_type=jnp.float32)

def renormed(weight, gradient):
    wide = weight.astype(jnp.float32)
    moved = wide - gradient
    factor = jnp.sqrt(lax.optimization_barrier(jnp.sum(wide * wide, axis=0))) / jnp.sqrt(lax.optimization_barrier(jnp.sum(moved * moved, axis=0)) + 1e-06)
    return (moved * factor[None, :]).astype(jnp.bfloat16)

def one_head(packed):
    query_head, key_head, value_head, rate_head, gate_w, down_w, up_w = packed
    gate_pre = jnp.dot(key_head, gate_w, preferred_element_type=jnp.float32)
    up_pre = jnp.dot(key_head, up_w, preferred_element_type=jnp.float32)
    sigma = jax.nn.sigmoid(gate_pre)
    hidden = (gate_pre * sigma * up_pre).astype(jnp.bfloat16)
    d_out = (-rate_head[:, None] * value_head.astype(jnp.float32)).astype(jnp.bfloat16)
    d_hidden = lax.dot_general(d_out, down_w, (((1,), (1,)), ((), ())), preferred_element_type=jnp.float32)
    d_gate = (d_hidden * up_pre * sigma * (1.0 + gate_pre * (1.0 - sigma))).astype(jnp.bfloat16)
    d_up = (d_hidden * gate_pre * sigma).astype(jnp.bfloat16)
    gate_new = renormed(gate_w, inner_sum(key_head, d_gate))
    down_new = renormed(down_w, inner_sum(hidden, d_out))
    up_new = renormed(up_w, inner_sum(key_head, d_up))
    first = jnp.dot(query_head, gate_new, preferred_element_type=jnp.float32)
    second = jnp.dot(query_head, up_new, preferred_element_type=jnp.float32)
    mixed = (first * jax.nn.sigmoid(first) * second).astype(jnp.bfloat16)
    result = jnp.dot(mixed, down_new, preferred_element_type=jnp.float32).astype(jnp.bfloat16)
    return (result, gate_new, down_new, up_new)

def reference(queries, keys, values, rates, gate_fast, down_fast, up_fast):
    count = queries.shape[0]

    def split_heads(array):
        return array.reshape(count, H, DH).transpose(1, 0, 2)
    result, gate_next, down_next, up_next = lax.map(one_head, (split_heads(queries), split_heads(keys), split_heads(values), rates.T, gate_fast, down_fast, up_fast))
    outputs = result.transpose(1, 0, 2).reshape(count, H * DH)
    return (outputs, gate_next, down_next, up_next)
```

```python
import functools

import jax
import jax.numpy as jnp
from jax import lax
from jax.experimental import pallas as pl
from jax.experimental.pallas import tpu as pltpu
from jax.sharding import PartitionSpec as P

MESH = pl.DeviceIdType.MESH
NX, NZ = 4, 8
ROWS = 128
WIDTH = 512
PAIR = 2 * WIDTH
MATS = 6
PIECE = WIDTH // (NX * NZ)

GROUPS = ((0, 2, "x"), (2, 1, "z"), (3, 3, "x"))


def dot(left, right, dims):
    return lax.dot_general(
        left, right, ((dims[:1], dims[1:]), ((), ())), preferred_element_type=jnp.float32
    )


def kernel(
    q_ref, k_ref, v_ref, rate_ref, gate_ref, down_ref, up_ref,
    out_ref, gate_out, down_out, up_out,
    d_own, k_all, d_all, q_all, hid, d_gate, d_up, grads, mixed, results, next_t,
    first_in, first_sum, second_in, second_sum, last_in,
    in_send, in_recv, red_send, red_recv, last_send, last_recv, gat_send, gat_recv,
    out_send, out_recv,
):
    group = lax.axis_index("heads")
    place = lax.axis_index("tokens")
    y_lo, core = group // 2, group % 2
    x, z, y_hi = place // 16, (place // 2) % 8, place % 2
    y = y_hi * 2 + y_lo

    def device(y, core, x, z):
        return ((y % 2) * 2 + core, (x * NZ + z) * 2 + y // 2)

    peers = {
        "x": [device(y, core, (x + step) % NX, z) for step in range(1, NX)],
        "z": [device(y, core, x, (z + step) % NZ) for step in range(1, NZ)],
    }
    position = {"x": x, "z": z}
    size = {"x": NX, "z": NZ}
    other = {"x": "z", "z": "x"}
    opposite = device((y + 2) % 4, core, x, z)
    sibling = device(y, 1 - core, x, z)
    forward = (y + 1 + 2 * core) % 4
    targets = [sibling, device(forward, 0, x, z), device(forward, 1, x, z)]
    below, above = device((y + 3) % 4, 0, x, z), device((y + 1) % 4, 1, x, z)
    sources = [sibling, below, above]
    target_group = [y_lo * 2 + 1 - core, (1 - y_lo) * 2, (1 - y_lo) * 2 + 1]
    target_slot = [1, 2 + core, 2 + core]
    source_group = [y_lo * 2 + 1 - core, (1 - y_lo) * 2, (1 - y_lo) * 2 + 1]

    barrier = pltpu.get_barrier_semaphore()
    greeted = peers["x"] + peers["z"] + [opposite] + targets + sources[1:]
    for peer in greeted:
        pl.semaphore_signal(barrier, inc=1, device_id=peer, device_id_type=MESH)

    for head in range(8):
        cols = slice(head * WIDTH, (head + 1) * WIDTH)
        d_own[:, cols] = (-rate_ref[:, head : head + 1] * v_ref[:, cols].astype(jnp.float32)).astype(
            jnp.bfloat16
        )
    pl.semaphore_wait(barrier, len(greeted))

    def columns(of_group, head):
        return pl.ds(pl.multiple_of(of_group * PAIR, PAIR) + head * WIDTH, WIDTH)

    def slot_rows(slot):
        if isinstance(slot, int):
            return pl.ds(slot * ROWS, ROWS)
        return pl.ds(pl.multiple_of(slot * ROWS, ROWS), ROWS)

    started = []

    def send(src, dst, send_sem, recv_sem, to):
        copy = pltpu.make_async_remote_copy(
            src_ref=src, dst_ref=dst, send_sem=send_sem, recv_sem=recv_sem,
            device_id=to, device_id_type=MESH,
        )
        copy.start()
        started.append(copy)
        return copy

    incoming = {}

    def exchange(which, src, dst, head):
        for n in (1, 2, 0):
            at = (which, head)
            if n == 0:
                recv_at = in_recv.at[which, head, 0]
            else:
                recv_at = in_recv.at[which, head, 1 + core]
            copy = send(
                src.at[:, columns(target_group[n], head)],
                dst.at[slot_rows(target_slot[n]), pl.ds(head * WIDTH, WIDTH)],
                in_send.at[which, head, n],
                recv_at,
                targets[n],
            )
        dst[slot_rows(0), pl.ds(head * WIDTH, WIDTH)] = src[:, columns(group, head)]

    def arrived(which, dst, head, n):
        there = dst.at[slot_rows(1 + n), pl.ds(head * WIDTH, WIDTH)]
        pltpu.make_async_remote_copy(
            src_ref=there, dst_ref=there, send_sem=in_send.at[which, head, n],
            recv_sem=in_recv.at[which, head, n], device_id=sources[n], device_id_type=MESH,
        ).wait_recv()

    for head in range(2):
        exchange(0, k_ref, k_all, head)
        exchange(1, d_own, d_all, head)

    def gradients(head):
        cols = slice(head * WIDTH, (head + 1) * WIDTH)
        for half in range(2):
            if half == 0:
                arrived(0, k_all, head, 0)
                arrived(1, d_all, head, 0)
            else:
                for n in (1, 2):
                    arrived(0, k_all, head, n)
                    arrived(1, d_all, head, n)
            rows = slice(half * 2 * ROWS, (half + 1) * 2 * ROWS)
            keys = k_all[rows, cols]
            d_out = d_all[rows, cols]
            gate_pre = dot(keys, gate_ref[head], (1, 0))
            up_pre = dot(keys, up_ref[head], (1, 0))
            d_hidden = dot(d_out, down_ref[head], (1, 1))
            sigma = jax.nn.sigmoid(gate_pre)
            silu = gate_pre * sigma
            hid[rows, :] = (silu * up_pre).astype(jnp.bfloat16)
            d_gate[rows, :] = (d_hidden * up_pre * sigma * (1.0 + gate_pre * (1.0 - sigma))).astype(
                jnp.bfloat16
            )
            d_up[rows, :] = (d_hidden * silu).astype(jnp.bfloat16)
        base = 3 * head
        grads[base] = dot(d_gate[...], k_all[:, cols], (0, 0)).astype(jnp.bfloat16)
        grads[base + 1] = dot(d_up[...], k_all[:, cols], (0, 0)).astype(jnp.bfloat16)
        grads[base + 2] = dot(d_all[:, cols], hid[...], (0, 0)).astype(jnp.bfloat16)

    def slab(axis, index, rows):
        return pl.ds(pl.multiple_of(index * rows, rows), rows)

    def reduce_start(g, level):
        first, count, axis = GROUPS[g]
        if level == 0:
            src, dst, rows = grads.at[first : first + count], first_in[g], WIDTH // size[axis]
        else:
            axis = other[axis]
            src, dst, rows = first_sum[g], second_in[g], PIECE
        for n, peer in enumerate(peers[axis]):
            index = (position[axis] + n + 1) % size[axis]
            incoming["reduce", g, level, n] = send(
                src.at[:, slab(axis, index, rows), :], dst.at[n],
                red_send.at[g, level, n], red_recv.at[g, level, n], peer,
            )

    def reduce_finish(g, level):
        first, count, axis = GROUPS[g]
        if level == 0:
            src, rows = grads.at[first : first + count], WIDTH // size[axis]
            dst, total = first_in[g], first_sum[g]
        else:
            axis = other[axis]
            src, rows = first_sum[g], PIECE
            dst, total = second_in[g], second_sum[g]
        for n in range(len(peers[axis])):
            incoming["reduce", g, level, n].wait_recv()
        for m in range(count):
            own = src[m, slab(axis, position[axis], rows), :].astype(jnp.float32)
            for n in range(len(peers[axis])):
                own = own + dst[n, m].astype(jnp.float32)
            total[m] = own.astype(jnp.bfloat16)

    def last_start(g):
        incoming["last", g] = send(
            second_sum[g], last_in[g], last_send.at[g], last_recv.at[g], opposite
        )

    def piece_start(g):
        axis = GROUPS[g][2]
        return position[axis] * (WIDTH // size[axis]) + position[other[axis]] * PIECE

    def renormed(g):
        first, count, axis = GROUPS[g]
        begin = piece_start(g)
        chosen = (
            lax.broadcasted_iota(jnp.int32, (PIECE, WIDTH), 1)
            == lax.broadcasted_iota(jnp.int32, (PIECE, WIDTH), 0) + begin
        )
        pick = jnp.where(chosen, 1.0, 0.0).astype(jnp.bfloat16)
        incoming["last", g].wait_recv()
        for m in range(count):
            head, kind = divmod(first + m, 3)
            weight = (gate_ref, up_ref, down_ref)[kind][head]
            wide = dot(pick, weight, (1, 1))
            total = second_sum[g][m].astype(jnp.float32) + last_in[g][m].astype(jnp.float32)
            moved = wide - total
            factor = jnp.sqrt(jnp.sum(wide * wide, axis=1, keepdims=True)) / jnp.sqrt(
                jnp.sum(moved * moved, axis=1, keepdims=True) + 1e-06
            )
            next_t[first + m, pl.ds(pl.multiple_of(begin, PIECE), PIECE), :] = (
                moved * factor
            ).astype(jnp.bfloat16)

    def gather_start(g, level):
        first, count, axis = GROUPS[g]
        if level == 0:
            axis = other[axis]
            begin, rows = piece_start(g), PIECE
        else:
            rows = WIDTH // size[axis]
            begin = position[axis] * rows
        here = next_t.at[first : first + count, pl.ds(pl.multiple_of(begin, rows), rows), :]
        for n, peer in enumerate(peers[axis]):
            incoming["gather", g, level, n] = send(
                here, here, gat_send.at[g, level, n], gat_recv.at[g, level, n], peer
            )

    def gather_finish(g, level):
        first, count, axis = GROUPS[g]
        if level == 0:
            axis = other[axis]
        for n in range(len(peers[axis])):
            incoming["gather", g, level, n].wait_recv()

    def of_head(head):
        return [g for g, (first, count, _) in enumerate(GROUPS) if first // 3 == head]

    for head in range(2):
        gradients(head)
        for g in of_head(head):
            reduce_start(g, 0)
        exchange(2, q_ref, q_all, head)
    everyone = range(len(GROUPS))
    for g in everyone:
        reduce_finish(g, 0)
        reduce_start(g, 1)
    for g in everyone:
        reduce_finish(g, 1)
        last_start(g)
    for g in everyone:
        renormed(g)
        gather_start(g, 0)
    for g in everyone:
        gather_finish(g, 0)
        gather_start(g, 1)

    for head in range(2):
        cols = slice(head * WIDTH, (head + 1) * WIDTH)
        for n in range(3):
            arrived(2, q_all, head, n)
        for g in of_head(head):
            gather_finish(g, 1)
        for half in (1, 0):
            rows = slice(half * 2 * ROWS, (half + 1) * 2 * ROWS)
            queries = q_all[rows, cols]
            first = dot(queries, next_t[3 * head], (1, 1))
            second = dot(queries, next_t[3 * head + 1], (1, 1))
            mixed[rows, :] = (first * jax.nn.sigmoid(first) * second).astype(jnp.bfloat16)
            results[rows, cols] = dot(mixed[rows, :], next_t[3 * head + 2], (1, 1)).astype(
                jnp.bfloat16
            )
            for n in ((1, 2) if half else (0,)):
                index = 0 if n == 0 else 1 + core
                send(
                    results.at[slot_rows(1 + n), cols], out_ref.at[:, columns(group, head)],
                    out_send.at[head, n], out_recv.at[head, index], sources[n],
                )
        out_ref[:, columns(group, head)] = results[slot_rows(0), cols]

    same = (
        lax.broadcasted_iota(jnp.int32, (WIDTH, WIDTH), 0)
        == lax.broadcasted_iota(jnp.int32, (WIDTH, WIDTH), 1)
    )
    unit = jnp.where(same, 1.0, 0.0).astype(jnp.bfloat16)
    for head in range(2):
        for kind, target in enumerate((gate_out, up_out, down_out)):
            target[head] = dot(unit, next_t[3 * head + kind], (1, 1)).astype(jnp.bfloat16)

    for head in range(2):
        for n in range(3):
            there = out_ref.at[:, columns(target_group[n], head)]
            pltpu.make_async_remote_copy(
                src_ref=there, dst_ref=there, send_sem=out_send.at[head, n],
                recv_sem=out_recv.at[head, n], device_id=targets[n], device_id_type=MESH,
            ).wait_recv()
    for copy in started:
        copy.wait_send()


def solution(mesh):
    def step(queries, keys, values, rates, gate_fast, down_fast, up_fast):
        size = {"x": NX, "z": NZ}
        bf16 = jnp.bfloat16

        def per_group(shape):
            return [pltpu.VMEM(shape(count, axis), bf16) for _, count, axis in GROUPS]

        slab = lambda axis: WIDTH // size[axis]
        rest = lambda axis: NX * NZ // size[axis]
        whole = pl.BlockSpec(memory_space=pltpu.VMEM)
        groups = len(GROUPS)
        return pl.pallas_call(
            kernel,
            out_shape=(
                jax.ShapeDtypeStruct(queries.shape, bf16),
                jax.ShapeDtypeStruct(gate_fast.shape, bf16),
                jax.ShapeDtypeStruct(down_fast.shape, bf16),
                jax.ShapeDtypeStruct(up_fast.shape, bf16),
            ),
            in_specs=[whole] * 7,
            out_specs=[whole] * 4,
            scratch_shapes=[
                pltpu.VMEM((ROWS, 8 * WIDTH), bf16),
                pltpu.VMEM((4 * ROWS, PAIR), bf16),
                pltpu.VMEM((4 * ROWS, PAIR), bf16),
                pltpu.VMEM((4 * ROWS, PAIR), bf16),
                pltpu.VMEM((4 * ROWS, WIDTH), bf16),
                pltpu.VMEM((4 * ROWS, WIDTH), bf16),
                pltpu.VMEM((4 * ROWS, WIDTH), bf16),
                pltpu.VMEM((MATS, WIDTH, WIDTH), bf16),
                pltpu.VMEM((4 * ROWS, WIDTH), bf16),
                pltpu.VMEM((4 * ROWS, PAIR), bf16),
                pltpu.VMEM((MATS, WIDTH, WIDTH), bf16),
                per_group(lambda count, axis: (size[axis] - 1, count, slab(axis), WIDTH)),
                per_group(lambda count, axis: (count, slab(axis), WIDTH)),
                per_group(lambda count, axis: (rest(axis) - 1, count, PIECE, WIDTH)),
                per_group(lambda count, axis: (count, PIECE, WIDTH)),
                per_group(lambda count, axis: (count, PIECE, WIDTH)),
                pltpu.SemaphoreType.DMA((3, 2, 3)),
                pltpu.SemaphoreType.DMA((3, 2, 3)),
                pltpu.SemaphoreType.DMA((groups, 2, NZ - 1)),
                pltpu.SemaphoreType.DMA((groups, 2, NZ - 1)),
                pltpu.SemaphoreType.DMA((groups,)),
                pltpu.SemaphoreType.DMA((groups,)),
                pltpu.SemaphoreType.DMA((groups, 2, NZ - 1)),
                pltpu.SemaphoreType.DMA((groups, 2, NZ - 1)),
                pltpu.SemaphoreType.DMA((2, 3)),
                pltpu.SemaphoreType.DMA((2, 3)),
            ],
            compiler_params=pltpu.CompilerParams(
                collective_id=0, has_side_effects=True, vmem_limit_bytes=56 << 20
            ),
        )(queries, keys, values, rates, gate_fast, down_fast, up_fast)

    tokens = P(("heads", "tokens"), None)
    weights = P("heads", None, None)
    return jax.shard_map(
        step,
        mesh=mesh,
        in_specs=(tokens,) * 4 + (weights,) * 3,
        out_specs=(tokens,) + (weights,) * 3,
        check_vma=False,
    )
```

```python
import functools

import jax
import jax.numpy as jnp
from jax import lax
from jax.experimental import pallas as pl
from jax.experimental.pallas import tpu as pltpu
from jax.sharding import PartitionSpec as P

MESH = pl.DeviceIdType.MESH
NX, NZ = 4, 8
ROWS = 128
WIDTH = 512
PAIR = 2 * WIDTH
MATS = 6
PIECE = WIDTH // (NX * NZ)

GROUPS = ((0, 2, "x"), (2, 1, "z"), (3, 2, "x"), (5, 1, "z"))


def dot(left, right, dims):
    return lax.dot_general(
        left, right, ((dims[:1], dims[1:]), ((), ())), preferred_element_type=jnp.float32
    )


def kernel(
    q_hbm, k_hbm, v_hbm, rate_hbm, gate_hbm, down_hbm, up_hbm,
    out_ref, next_t,
    v_ref, rate_ref, gate_ref, down_ref, up_ref,
    d_own, k_all, d_all, q_all, hid, d_gate, d_up, grads, mixed, results,
    first_in, first_sum, second_in, second_sum, last_in,
    local_sem, in_send, in_recv, red_send, red_recv, last_send, last_recv,
    gat_send, gat_recv, for_send, for_recv, out_send, out_recv,
):
    group = lax.axis_index("heads")
    place = lax.axis_index("tokens")
    y_lo, core = group // 2, group % 2
    x, z, y_hi = place // 16, (place // 2) % 8, place % 2
    y = y_hi * 2 + y_lo

    def device(y, core, x, z):
        return ((y % 2) * 2 + core, (x * NZ + z) * 2 + y // 2)

    peers = {
        "x": [device(y, core, (x + step) % NX, z) for step in range(1, NX)],
        "z": [device(y, core, x, (z + step) % NZ) for step in range(1, NZ)],
    }
    position = {"x": x, "z": z}
    size = {"x": NX, "z": NZ}
    other = {"x": "z", "z": "x"}
    opposite = device((y + 2) % 4, core, x, z)
    sibling = device(y, 1 - core, x, z)
    forward = (y + 1 + 2 * core) % 4
    targets = [sibling, device(forward, 0, x, z), device(forward, 1, x, z)]
    below, above = device((y + 3) % 4, 0, x, z), device((y + 1) % 4, 1, x, z)
    sources = [sibling, below, above]
    target_group = [y_lo * 2 + 1 - core, (1 - y_lo) * 2, (1 - y_lo) * 2 + 1]
    target_slot = [1, 2 + core, 2 + core]
    source_group = [y_lo * 2 + 1 - core, (1 - y_lo) * 2, (1 - y_lo) * 2 + 1]

    barrier = pltpu.get_barrier_semaphore()
    greeted = peers["x"] + peers["z"] + [opposite] + targets + sources[1:]
    for peer in greeted:
        pl.semaphore_signal(barrier, inc=1, device_id=peer, device_id_type=MESH)

    def columns(of_group, head):
        return pl.ds(pl.multiple_of(of_group * PAIR, PAIR) + head * WIDTH, WIDTH)

    def slot_rows(slot):
        if isinstance(slot, int):
            return pl.ds(slot * ROWS, ROWS)
        return pl.ds(pl.multiple_of(slot * ROWS, ROWS), ROWS)

    started = []

    def send(src, dst, send_sem, recv_sem, to):
        copy = pltpu.make_async_remote_copy(
            src_ref=src, dst_ref=dst, send_sem=send_sem, recv_sem=recv_sem,
            device_id=to, device_id_type=MESH,
        )
        copy.start()
        started.append(copy)
        return copy

    incoming = {}

    def local(src, dst, index):
        copy = pltpu.make_async_copy(src, dst, local_sem.at[index])
        copy.start()
        return copy

    own_cols = pl.ds(pl.multiple_of(group * PAIR, PAIR), PAIR)
    loads = {
        name: local(src, dst, index)
        for index, (name, src, dst) in enumerate(
            (
                ("rate", rate_hbm, rate_ref),
                ("value", v_hbm, v_ref),
                ("key", k_hbm.at[:, own_cols], k_all.at[slot_rows(0), :]),
                ("gate", gate_hbm, gate_ref),
                ("up", up_hbm, up_ref),
                ("down", down_hbm, down_ref),
                ("query", q_hbm.at[:, own_cols], q_all.at[slot_rows(0), :]),
            )
        )
    }

    loads["rate"].wait()
    rate_cols = jnp.transpose(rate_ref[...])
    loads["value"].wait()
    for head in range(8):
        cols = slice(head * WIDTH, (head + 1) * WIDTH)
        d_own[:, cols] = (-rate_cols[:, head : head + 1] * v_ref[:, cols].astype(jnp.float32)).astype(
            jnp.bfloat16
        )

    pl.semaphore_wait(barrier, len(greeted))

    def exchange(which, src, dst, head):
        for n in (1, 2, 0):
            index = 0 if n == 0 else 1 + core
            send(
                src.at[:, columns(target_group[n], head)],
                dst.at[slot_rows(target_slot[n]), pl.ds(head * WIDTH, WIDTH)],
                in_send.at[which, head, n], in_recv.at[which, head, index], targets[n],
            )

    def arrived(which, dst, head, n):
        there = dst.at[slot_rows(1 + n), pl.ds(head * WIDTH, WIDTH)]
        pltpu.make_async_remote_copy(
            src_ref=there, dst_ref=there, send_sem=in_send.at[which, head, n],
            recv_sem=in_recv.at[which, head, n], device_id=sources[n], device_id_type=MESH,
        ).wait_recv()

    for head in range(2):
        exchange(0, k_hbm, k_all, head)
        exchange(1, d_own, d_all, head)
    d_all[slot_rows(0), :] = d_own[:, own_cols]
    for name in ("key", "gate", "up", "down"):
        loads[name].wait()

    def gradients(head):
        cols = slice(head * WIDTH, (head + 1) * WIDTH)
        for half in range(2):
            if half == 0:
                arrived(0, k_all, head, 0)
                arrived(1, d_all, head, 0)
            else:
                for n in (1, 2):
                    arrived(0, k_all, head, n)
                    arrived(1, d_all, head, n)
            rows = slice(half * 2 * ROWS, (half + 1) * 2 * ROWS)
            keys = k_all[rows, cols]
            d_out = d_all[rows, cols]
            gate_pre = dot(keys, gate_ref[head], (1, 0))
            up_pre = dot(keys, up_ref[head], (1, 0))
            d_hidden = dot(d_out, down_ref[head], (1, 1))
            sigma = jax.nn.sigmoid(gate_pre)
            silu = gate_pre * sigma
            hid[rows, :] = (silu * up_pre).astype(jnp.bfloat16)
            d_gate[rows, :] = (d_hidden * up_pre * sigma * (1.0 + gate_pre * (1.0 - sigma))).astype(
                jnp.bfloat16
            )
            d_up[rows, :] = (d_hidden * silu).astype(jnp.bfloat16)
        base = 3 * head
        grads[base + 2] = dot(d_all[:, cols], hid[...], (0, 0)).astype(jnp.bfloat16)
        reduce_start(2 * head + 1, 0)
        grads[base] = dot(d_gate[...], k_all[:, cols], (0, 0)).astype(jnp.bfloat16)
        grads[base + 1] = dot(d_up[...], k_all[:, cols], (0, 0)).astype(jnp.bfloat16)
        reduce_start(2 * head, 0)

    def slab(axis, index, rows):
        return pl.ds(pl.multiple_of(index * rows, rows), rows)

    def reduce_start(g, level):
        first, count, axis = GROUPS[g]
        if level == 0:
            src, dst, rows = grads.at[first : first + count], first_in[g], WIDTH // size[axis]
        else:
            axis = other[axis]
            src, dst, rows = first_sum[g], second_in[g], PIECE
        for n, peer in enumerate(peers[axis]):
            index = (position[axis] + n + 1) % size[axis]
            incoming["reduce", g, level, n] = send(
                src.at[:, slab(axis, index, rows), :], dst.at[n],
                red_send.at[g, level, n], red_recv.at[g, level, n], peer,
            )

    def reduce_finish(g, level):
        first, count, axis = GROUPS[g]
        if level == 0:
            src, rows = grads.at[first : first + count], WIDTH // size[axis]
            dst, total = first_in[g], first_sum[g]
        else:
            axis = other[axis]
            src, rows = first_sum[g], PIECE
            dst, total = second_in[g], second_sum[g]
        for n in range(len(peers[axis])):
            incoming["reduce", g, level, n].wait_recv()
        for m in range(count):
            own = src[m, slab(axis, position[axis], rows), :].astype(jnp.float32)
            for n in range(len(peers[axis])):
                own = own + dst[n, m].astype(jnp.float32)
            total[m] = own.astype(jnp.bfloat16)

    def last_start(g):
        incoming["last", g] = send(
            second_sum[g], last_in[g], last_send.at[g], last_recv.at[g], opposite
        )

    def piece_start(g):
        axis = GROUPS[g][2]
        return position[axis] * (WIDTH // size[axis]) + position[other[axis]] * PIECE

    def renormed(g):
        first, count, axis = GROUPS[g]
        begin = piece_start(g)
        chosen = (
            lax.broadcasted_iota(jnp.int32, (PIECE, WIDTH), 1)
            == lax.broadcasted_iota(jnp.int32, (PIECE, WIDTH), 0) + begin
        )
        pick = jnp.where(chosen, 1.0, 0.0).astype(jnp.bfloat16)
        incoming["last", g].wait_recv()
        for m in range(count):
            head, kind = divmod(first + m, 3)
            weight = (gate_ref, up_ref, down_ref)[kind][head]
            wide = dot(pick, weight, (1, 1))
            total = second_sum[g][m].astype(jnp.float32) + last_in[g][m].astype(jnp.float32)
            moved = wide - total
            factor = jnp.sqrt(jnp.sum(wide * wide, axis=1, keepdims=True)) / jnp.sqrt(
                jnp.sum(moved * moved, axis=1, keepdims=True) + 1e-06
            )
            next_t[first + m, pl.ds(pl.multiple_of(begin, PIECE), PIECE), :] = (
                moved * factor
            ).astype(jnp.bfloat16)

    def piece(g, index):
        first, count, axis = GROUPS[g]
        begin = position[axis] * (WIDTH // size[axis]) + index * PIECE
        return next_t.at[first : first + count, pl.ds(pl.multiple_of(begin, PIECE), PIECE), :]

    def forward_piece(g, index):
        for n, peer in enumerate(peers[GROUPS[g][2]]):
            pltpu.make_async_remote_copy(
                src_ref=piece(g, index), dst_ref=piece(g, index),
                send_sem=for_send.at[g, n], recv_sem=for_recv.at[g, n],
                device_id=peer, device_id_type=MESH,
            ).start()

    def gather_start(g):
        axis = other[GROUPS[g][2]]
        here = piece(g, position[axis])
        for n, peer in enumerate(peers[axis]):
            incoming["gather", g, n] = send(here, here, gat_send.at[g, n], gat_recv.at[g, n], peer)
        forward_piece(g, position[axis])

    def gather_forward(g):
        axis = other[GROUPS[g][2]]
        for n in range(len(peers[axis])):
            incoming["gather", g, n].wait_recv()
            forward_piece(g, (position[axis] + size[axis] - n - 1) % size[axis])

    def whole_slab(g, n):
        first, count, axis = GROUPS[g]
        here = next_t.at[first : first + count, slab(axis, position[axis], WIDTH // size[axis]), :]
        return pltpu.make_async_remote_copy(
            src_ref=here, dst_ref=here, send_sem=for_send.at[g, n], recv_sem=for_recv.at[g, n],
            device_id=peers[axis][n], device_id_type=MESH,
        )

    def gather_finish(g):
        for n in range(len(peers[GROUPS[g][2]])):
            whole_slab(g, n).wait_recv()

    def of_head(head):
        return [g for g, (first, count, _) in enumerate(GROUPS) if first // 3 == head]

    for head in range(2):
        gradients(head)
    for head in range(2):
        exchange(2, q_hbm, q_all, head)
    everyone = range(len(GROUPS))
    for g in everyone:
        reduce_finish(g, 0)
        reduce_start(g, 1)
    for g in everyone:
        reduce_finish(g, 1)
        last_start(g)
    for g in everyone:
        renormed(g)
        gather_start(g)
    for g in everyone:
        gather_forward(g)
    loads["query"].wait()

    for head in range(2):
        cols = slice(head * WIDTH, (head + 1) * WIDTH)
        for n in range(3):
            arrived(2, q_all, head, n)
        for g in of_head(head):
            gather_finish(g)
        for half in (1, 0):
            rows = slice(half * 2 * ROWS, (half + 1) * 2 * ROWS)
            queries = q_all[rows, cols]
            first = dot(queries, next_t[3 * head], (1, 1))
            second = dot(queries, next_t[3 * head + 1], (1, 1))
            mixed[rows, :] = (first * jax.nn.sigmoid(first) * second).astype(jnp.bfloat16)
            results[rows, cols] = dot(mixed[rows, :], next_t[3 * head + 2], (1, 1)).astype(
                jnp.bfloat16
            )
            for n in ((1, 2) if half else (0,)):
                index = 0 if n == 0 else 1 + core
                send(
                    results.at[slot_rows(1 + n), cols], out_ref.at[:, columns(group, head)],
                    out_send.at[head, n], out_recv.at[head, index], sources[n],
                )
        out_ref[:, columns(group, head)] = results[slot_rows(0), cols]

    for head in range(2):
        for n in range(3):
            there = out_ref.at[:, columns(target_group[n], head)]
            pltpu.make_async_remote_copy(
                src_ref=there, dst_ref=there, send_sem=out_send.at[head, n],
                recv_sem=out_recv.at[head, n], device_id=targets[n], device_id_type=MESH,
            ).wait_recv()
    for copy in started:
        copy.wait_send()
    for g in everyone:
        for n in range(len(peers[GROUPS[g][2]])):
            whole_slab(g, n).wait_send()


def finish(staged, next_t, out_ref, gate_ref, down_ref, up_ref, turned, sems):
    copies = [pltpu.make_async_copy(staged, out_ref, sems.at[MATS])]
    copies[0].start()
    same = (
        lax.broadcasted_iota(jnp.int32, (WIDTH, WIDTH), 0)
        == lax.broadcasted_iota(jnp.int32, (WIDTH, WIDTH), 1)
    )
    unit = jnp.where(same, 1.0, 0.0).astype(jnp.bfloat16)
    for m in range(MATS):
        head, kind = divmod(m, 3)
        turned[m] = dot(unit, next_t[m], (1, 1)).astype(jnp.bfloat16)
        copy = pltpu.make_async_copy(
            turned.at[m], (gate_ref, up_ref, down_ref)[kind].at[head], sems.at[m]
        )
        copy.start()
        copies.append(copy)
    for copy in copies:
        copy.wait()


def solution(mesh):
    def step(queries, keys, values, rates, gate_fast, down_fast, up_fast):
        size = {"x": NX, "z": NZ}
        bf16 = jnp.bfloat16

        def per_group(shape):
            return [pltpu.VMEM(shape(count, axis), bf16) for _, count, axis in GROUPS]

        slab = lambda axis: WIDTH // size[axis]
        rest = lambda axis: NX * NZ // size[axis]
        vmem = pl.BlockSpec(memory_space=pltpu.VMEM)
        anywhere = pl.BlockSpec(memory_space=pltpu.HBM)
        groups = len(GROUPS)
        weight = gate_fast.shape
        outs = (
            jax.ShapeDtypeStruct(queries.shape, bf16),
            jax.ShapeDtypeStruct(weight, bf16),
            jax.ShapeDtypeStruct(weight, bf16),
            jax.ShapeDtypeStruct(weight, bf16),
        )
        staged, next_t = pl.pallas_call(
            kernel,
            out_shape=(
                pltpu.VMEM(queries.shape, bf16),
                pltpu.VMEM((MATS, WIDTH, WIDTH), bf16),
            ),
            in_specs=[anywhere] * 7,
            out_specs=[vmem] * 2,
            scratch_shapes=[
                pltpu.VMEM((ROWS, 8 * WIDTH), bf16),
                pltpu.VMEM((8, ROWS), jnp.float32),
                pltpu.VMEM(weight, bf16),
                pltpu.VMEM(weight, bf16),
                pltpu.VMEM(weight, bf16),
                pltpu.VMEM((ROWS, 8 * WIDTH), bf16),
                pltpu.VMEM((4 * ROWS, PAIR), bf16),
                pltpu.VMEM((4 * ROWS, PAIR), bf16),
                pltpu.VMEM((4 * ROWS, PAIR), bf16),
                pltpu.VMEM((4 * ROWS, WIDTH), bf16),
                pltpu.VMEM((4 * ROWS, WIDTH), bf16),
                pltpu.VMEM((4 * ROWS, WIDTH), bf16),
                pltpu.VMEM((MATS, WIDTH, WIDTH), bf16),
                pltpu.VMEM((4 * ROWS, WIDTH), bf16),
                pltpu.VMEM((4 * ROWS, PAIR), bf16),
                per_group(lambda count, axis: (size[axis] - 1, count, slab(axis), WIDTH)),
                per_group(lambda count, axis: (count, slab(axis), WIDTH)),
                per_group(lambda count, axis: (rest(axis) - 1, count, PIECE, WIDTH)),
                per_group(lambda count, axis: (count, PIECE, WIDTH)),
                per_group(lambda count, axis: (count, PIECE, WIDTH)),
                pltpu.SemaphoreType.DMA((7,)),
                pltpu.SemaphoreType.DMA((3, 2, 3)),
                pltpu.SemaphoreType.DMA((3, 2, 3)),
                pltpu.SemaphoreType.DMA((groups, 2, NZ - 1)),
                pltpu.SemaphoreType.DMA((groups, 2, NZ - 1)),
                pltpu.SemaphoreType.DMA((groups,)),
                pltpu.SemaphoreType.DMA((groups,)),
                pltpu.SemaphoreType.DMA((groups, NZ - 1)),
                pltpu.SemaphoreType.DMA((groups, NZ - 1)),
                pltpu.SemaphoreType.DMA((groups, NZ - 1)),
                pltpu.SemaphoreType.DMA((groups, NZ - 1)),
                pltpu.SemaphoreType.DMA((2, 3)),
                pltpu.SemaphoreType.DMA((2, 3)),
            ],
            compiler_params=pltpu.CompilerParams(
                collective_id=0, has_side_effects=True, vmem_limit_bytes=40 << 20
            ),
        )(
            *(
                pltpu.with_memory_space_constraint(array, pltpu.HBM)
                for array in (queries, keys, values, rates.T, gate_fast, down_fast, up_fast)
            )
        )
        return pl.pallas_call(
            finish,
            out_shape=outs,
            in_specs=[vmem] * 2,
            out_specs=[anywhere] * 4,
            scratch_shapes=[
                pltpu.VMEM((MATS, WIDTH, WIDTH), bf16),
                pltpu.SemaphoreType.DMA((MATS + 1,)),
            ],
            compiler_params=pltpu.CompilerParams(vmem_limit_bytes=12 << 20),
        )(staged, next_t)

    tokens = P(("heads", "tokens"), None)
    weights = P("heads", None, None)
    return jax.shard_map(
        step,
        mesh=mesh,
        in_specs=(tokens,) * 4 + (weights,) * 3,
        out_specs=(tokens,) + (weights,) * 3,
        check_vma=False,
    )
```

```python
import functools

import jax
import jax.numpy as jnp
from jax import lax
from jax.experimental import pallas as pl
from jax.experimental.pallas import tpu as pltpu
from jax.sharding import PartitionSpec as P

MESH = pl.DeviceIdType.MESH
NX, NZ = 4, 8
ROWS = 128
WIDTH = 512
PAIR = 2 * WIDTH
MATS = 6
PIECE = WIDTH // (NX * NZ)

GROUPS = ((0, 2, "x", False), (2, 1, "z", False), (3, 2, "x", True), (5, 1, "x", False))
PAIRED = 2


def dot(left, right, dims):
    return lax.dot_general(
        left, right, ((dims[:1], dims[1:]), ((), ())), preferred_element_type=jnp.float32
    )


def kernel(
    q_hbm, k_hbm, v_hbm, rate_hbm, gate_hbm, down_hbm, up_hbm,
    out_ref, next_t,
    v_ref, rate_ref, gate_ref, down_ref, up_ref,
    d_own, k_all, d_all, q_all, hid, d_gate, d_up, grads, mixed, results,
    first_in, first_sum, second_in, second_sum, last_in,
    local_sem, in_send, in_recv, red_send, red_recv, last_send, last_recv,
    gat_send, gat_recv, for_send, for_recv, out_send, out_recv,
    pair_in, pair_sum, pair_send, pair_recv,
):
    group = lax.axis_index("heads")
    place = lax.axis_index("tokens")
    y_lo, core = group // 2, group % 2
    x, z, y_hi = place // 16, (place // 2) % 8, place % 2
    y = y_hi * 2 + y_lo

    def device(y, core, x, z):
        return ((y % 2) * 2 + core, (x * NZ + z) * 2 + y // 2)

    peers = {
        "x": [device(y, core, (x + step) % NX, z) for step in range(1, NX)],
        "z": [device(y, core, x, (z + step) % NZ) for step in range(1, NZ)],
    }
    position = {"x": x, "z": z}
    size = {"x": NX, "z": NZ}
    other = {"x": "z", "z": "x"}
    opposite = device((y + 2) % 4, core, x, z)
    sibling = device(y, 1 - core, x, z)
    forward = (y + 1 + 2 * core) % 4
    targets = [sibling, device(forward, 0, x, z), device(forward, 1, x, z)]
    below, above = device((y + 3) % 4, 0, x, z), device((y + 1) % 4, 1, x, z)
    sources = [sibling, below, above]
    target_group = [y_lo * 2 + 1 - core, (1 - y_lo) * 2, (1 - y_lo) * 2 + 1]
    target_slot = [1, 2 + core, 2 + core]
    source_group = [y_lo * 2 + 1 - core, (1 - y_lo) * 2, (1 - y_lo) * 2 + 1]

    barrier = pltpu.get_barrier_semaphore()
    greeted = peers["x"] + peers["z"] + [opposite] + targets + sources[1:]
    for peer in greeted:
        pl.semaphore_signal(barrier, inc=1, device_id=peer, device_id_type=MESH)

    def columns(of_group, head):
        return pl.ds(pl.multiple_of(of_group * PAIR, PAIR) + head * WIDTH, WIDTH)

    def slot_rows(slot):
        if isinstance(slot, int):
            return pl.ds(slot * ROWS, ROWS)
        return pl.ds(pl.multiple_of(slot * ROWS, ROWS), ROWS)

    started = []

    def send(src, dst, send_sem, recv_sem, to):
        copy = pltpu.make_async_remote_copy(
            src_ref=src, dst_ref=dst, send_sem=send_sem, recv_sem=recv_sem,
            device_id=to, device_id_type=MESH,
        )
        copy.start()
        started.append(copy)
        return copy

    incoming = {}

    def local(src, dst, index):
        copy = pltpu.make_async_copy(src, dst, local_sem.at[index])
        copy.start()
        return copy

    own_cols = pl.ds(pl.multiple_of(group * PAIR, PAIR), PAIR)
    loads = {
        name: local(src, dst, index)
        for index, (name, src, dst) in enumerate(
            (
                ("rate", rate_hbm, rate_ref),
                ("value", v_hbm, v_ref),
                ("key", k_hbm.at[:, own_cols], k_all.at[slot_rows(0), :]),
                ("gate", gate_hbm, gate_ref),
                ("up", up_hbm, up_ref),
                ("down", down_hbm, down_ref),
                ("query", q_hbm.at[:, own_cols], q_all.at[slot_rows(0), :]),
            )
        )
    }

    loads["rate"].wait()
    rate_cols = jnp.transpose(rate_ref[...])
    loads["value"].wait()
    for head in range(8):
        cols = slice(head * WIDTH, (head + 1) * WIDTH)
        d_own[:, cols] = (-rate_cols[:, head : head + 1] * v_ref[:, cols].astype(jnp.float32)).astype(
            jnp.bfloat16
        )

    pl.semaphore_wait(barrier, len(greeted))

    def exchange(which, src, dst, head):
        for n in (1, 2, 0):
            index = 0 if n == 0 else 1 + core
            send(
                src.at[:, columns(target_group[n], head)],
                dst.at[slot_rows(target_slot[n]), pl.ds(head * WIDTH, WIDTH)],
                in_send.at[which, head, n], in_recv.at[which, head, index], targets[n],
            )

    def arrived(which, dst, head, n):
        there = dst.at[slot_rows(1 + n), pl.ds(head * WIDTH, WIDTH)]
        pltpu.make_async_remote_copy(
            src_ref=there, dst_ref=there, send_sem=in_send.at[which, head, n],
            recv_sem=in_recv.at[which, head, n], device_id=sources[n], device_id_type=MESH,
        ).wait_recv()

    for head in range(2):
        exchange(0, k_hbm, k_all, head)
        exchange(1, d_own, d_all, head)
    d_all[slot_rows(0), :] = d_own[:, own_cols]
    for name in ("key", "gate", "up", "down"):
        loads[name].wait()

    def gradients(head):
        cols = slice(head * WIDTH, (head + 1) * WIDTH)
        for half in range(2):
            if half == 0:
                arrived(0, k_all, head, 0)
                arrived(1, d_all, head, 0)
            else:
                for n in (1, 2):
                    arrived(0, k_all, head, n)
                    arrived(1, d_all, head, n)
            rows = slice(half * 2 * ROWS, (half + 1) * 2 * ROWS)
            keys = k_all[rows, cols]
            d_out = d_all[rows, cols]
            gate_pre = dot(keys, gate_ref[head], (1, 0))
            up_pre = dot(keys, up_ref[head], (1, 0))
            d_hidden = dot(d_out, down_ref[head], (1, 1))
            sigma = jax.nn.sigmoid(gate_pre)
            silu = gate_pre * sigma
            hid[rows, :] = (silu * up_pre).astype(jnp.bfloat16)
            d_gate[rows, :] = (d_hidden * up_pre * sigma * (1.0 + gate_pre * (1.0 - sigma))).astype(
                jnp.bfloat16
            )
            d_up[rows, :] = (d_hidden * silu).astype(jnp.bfloat16)
        base = 3 * head
        if head == 0:
            grads[base + 2] = dot(d_all[:, cols], hid[...], (0, 0)).astype(jnp.bfloat16)
            reduce_start(1, 0)
        grads[base] = dot(d_gate[...], k_all[:, cols], (0, 0)).astype(jnp.bfloat16)
        grads[base + 1] = dot(d_up[...], k_all[:, cols], (0, 0)).astype(jnp.bfloat16)
        if head == 0:
            reduce_start(0, 0)
        else:
            pair_start()
            grads[base + 2] = dot(d_all[:, cols], hid[...], (0, 0)).astype(jnp.bfloat16)
            reduce_start(3, 0)

    def slab(axis, index, rows):
        return pl.ds(pl.multiple_of(index * rows, rows), rows)

    def matrices(g):
        first, count, _, paired = GROUPS[g]
        return pl.ds(first + y_hi, 1) if paired else pl.ds(first, count)

    def pair_start():
        first = GROUPS[PAIRED][0]
        incoming["pair"] = send(
            grads.at[first + 1 - y_hi], pair_in, pair_send.at[0], pair_recv.at[0], opposite
        )

    def pair_finish():
        first = GROUPS[PAIRED][0]
        incoming["pair"].wait_recv()
        pair_sum[0] = (
            grads[first + y_hi].astype(jnp.float32) + pair_in[...].astype(jnp.float32)
        ).astype(jnp.bfloat16)

    def reduce_buffers(g, level):
        _, count, axis, paired = GROUPS[g]
        if level == 0:
            src = pair_sum if paired else grads.at[matrices(g)]
            return src, first_in[g], first_sum[g], axis, WIDTH // size[axis]
        return first_sum[g], second_in[g], second_sum[g], other[axis], PIECE

    def reduce_start(g, level):
        src, dst, _, axis, rows = reduce_buffers(g, level)
        for n, peer in enumerate(peers[axis]):
            index = (position[axis] + n + 1) % size[axis]
            incoming["reduce", g, level, n] = send(
                src.at[:, slab(axis, index, rows), :], dst.at[n],
                red_send.at[g, level, n], red_recv.at[g, level, n], peer,
            )

    def reduce_finish(g, level):
        src, dst, total, axis, rows = reduce_buffers(g, level)
        for n in range(len(peers[axis])):
            incoming["reduce", g, level, n].wait_recv()
        for m in range(total.shape[0]):
            own = src[m, slab(axis, position[axis], rows), :].astype(jnp.float32)
            for n in range(len(peers[axis])):
                own = own + dst[n, m].astype(jnp.float32)
            total[m] = own.astype(jnp.bfloat16)

    def last_start(g):
        incoming["last", g] = send(
            second_sum[g], last_in[g], last_send.at[g], last_recv.at[g], opposite
        )

    def renormed(g):
        first, count, axis, paired = GROUPS[g]
        begin = position[axis] * (WIDTH // size[axis]) + position[other[axis]] * PIECE
        chosen = (
            lax.broadcasted_iota(jnp.int32, (PIECE, WIDTH), 1)
            == lax.broadcasted_iota(jnp.int32, (PIECE, WIDTH), 0) + begin
        )
        pick = jnp.where(chosen, 1.0, 0.0).astype(jnp.bfloat16)

        def old(m):
            head, kind = divmod(m, 3)
            return dot(pick, (gate_ref, up_ref, down_ref)[kind][head], (1, 1))

        if not paired:
            incoming["last", g].wait_recv()
        for m in range(1 if paired else count):
            total = second_sum[g][m].astype(jnp.float32)
            if paired:
                wide = jnp.where(y_hi == 0, old(first), old(first + 1))
            else:
                wide = old(first + m)
                total = total + last_in[g][m].astype(jnp.float32)
            moved = wide - total
            factor = jnp.sqrt(jnp.sum(wide * wide, axis=1, keepdims=True)) / jnp.sqrt(
                jnp.sum(moved * moved, axis=1, keepdims=True) + 1e-06
            )
            index = first + y_hi if paired else first + m
            next_t[index, pl.ds(pl.multiple_of(begin, PIECE), PIECE), :] = (moved * factor).astype(
                jnp.bfloat16
            )

    def piece(g, index):
        axis = GROUPS[g][2]
        begin = position[axis] * (WIDTH // size[axis]) + index * PIECE
        return next_t.at[matrices(g), pl.ds(pl.multiple_of(begin, PIECE), PIECE), :]

    def forward_piece(g, index):
        for n, peer in enumerate(peers[GROUPS[g][2]]):
            pltpu.make_async_remote_copy(
                src_ref=piece(g, index), dst_ref=piece(g, index),
                send_sem=for_send.at[g, n], recv_sem=for_recv.at[g, n],
                device_id=peer, device_id_type=MESH,
            ).start()

    def gather_start(g):
        axis = other[GROUPS[g][2]]
        here = piece(g, position[axis])
        for n, peer in enumerate(peers[axis]):
            incoming["gather", g, n] = send(here, here, gat_send.at[g, n], gat_recv.at[g, n], peer)
        forward_piece(g, position[axis])

    def gather_forward(g):
        axis = other[GROUPS[g][2]]
        for n in range(len(peers[axis])):
            incoming["gather", g, n].wait_recv()
            forward_piece(g, (position[axis] + size[axis] - n - 1) % size[axis])

    def whole_slab(g, n):
        axis = GROUPS[g][2]
        here = next_t.at[matrices(g), slab(axis, position[axis], WIDTH // size[axis]), :]
        return pltpu.make_async_remote_copy(
            src_ref=here, dst_ref=here, send_sem=for_send.at[g, n], recv_sem=for_recv.at[g, n],
            device_id=peers[axis][n], device_id_type=MESH,
        )

    def gather_finish(g):
        for n in range(len(peers[GROUPS[g][2]])):
            whole_slab(g, n).wait_recv()

    def share_slab(index):
        here = next_t.at[matrices(PAIRED), slab("x", index, WIDTH // NX), :]
        pltpu.make_async_remote_copy(
            src_ref=here, dst_ref=here, send_sem=pair_send.at[1], recv_sem=pair_recv.at[1],
            device_id=opposite, device_id_type=MESH,
        ).start()

    def share():
        share_slab(x)
        for n in range(NX - 1):
            whole_slab(PAIRED, n).wait_recv()
            share_slab((x + NX - n - 1) % NX)

    def shared():
        here = next_t.at[matrices(PAIRED)]
        return pltpu.make_async_remote_copy(
            src_ref=here, dst_ref=here, send_sem=pair_send.at[1], recv_sem=pair_recv.at[1],
            device_id=opposite, device_id_type=MESH,
        )

    for head in range(2):
        gradients(head)
    for head in range(2):
        exchange(2, q_hbm, q_all, head)
    for g in (0, 1, 2, 3):
        if g == PAIRED:
            pair_finish()
        else:
            reduce_finish(g, 0)
        reduce_start(g, 0 if g == PAIRED else 1)
    for g in (0, 1, 2, 3):
        if g == PAIRED:
            reduce_finish(g, 0)
            reduce_start(g, 1)
        else:
            reduce_finish(g, 1)
            last_start(g)
    for g in (0, 1, 3):
        renormed(g)
        gather_start(g)
    reduce_finish(PAIRED, 1)
    renormed(PAIRED)
    gather_start(PAIRED)
    for g in (0, 1, 3, 2):
        gather_forward(g)
    share()
    loads["query"].wait()

    for head in range(2):
        cols = slice(head * WIDTH, (head + 1) * WIDTH)
        for n in range(3):
            arrived(2, q_all, head, n)
        if head == 0:
            gather_finish(0)
            gather_finish(1)
        else:
            gather_finish(3)
            shared().wait_recv()
        for half in (1, 0):
            rows = slice(half * 2 * ROWS, (half + 1) * 2 * ROWS)
            queries = q_all[rows, cols]
            first = dot(queries, next_t[3 * head], (1, 1))
            second = dot(queries, next_t[3 * head + 1], (1, 1))
            mixed[rows, :] = (first * jax.nn.sigmoid(first) * second).astype(jnp.bfloat16)
            results[rows, cols] = dot(mixed[rows, :], next_t[3 * head + 2], (1, 1)).astype(
                jnp.bfloat16
            )
            for n in ((1, 2) if half else (0,)):
                index = 0 if n == 0 else 1 + core
                send(
                    results.at[slot_rows(1 + n), cols], out_ref.at[:, columns(group, head)],
                    out_send.at[head, n], out_recv.at[head, index], sources[n],
                )
        out_ref[:, columns(group, head)] = results[slot_rows(0), cols]

    for head in range(2):
        for n in range(3):
            there = out_ref.at[:, columns(target_group[n], head)]
            pltpu.make_async_remote_copy(
                src_ref=there, dst_ref=there, send_sem=out_send.at[head, n],
                recv_sem=out_recv.at[head, n], device_id=targets[n], device_id_type=MESH,
            ).wait_recv()
    for copy in started:
        copy.wait_send()
    shared().wait_send()
    for g in range(len(GROUPS)):
        for n in range(len(peers[GROUPS[g][2]])):
            whole_slab(g, n).wait_send()


def finish(staged, next_t, out_ref, gate_ref, down_ref, up_ref, turned, sems):
    copies = [pltpu.make_async_copy(staged, out_ref, sems.at[MATS])]
    copies[0].start()
    same = (
        lax.broadcasted_iota(jnp.int32, (WIDTH, WIDTH), 0)
        == lax.broadcasted_iota(jnp.int32, (WIDTH, WIDTH), 1)
    )
    unit = jnp.where(same, 1.0, 0.0).astype(jnp.bfloat16)
    for m in range(MATS):
        head, kind = divmod(m, 3)
        turned[m] = dot(unit, next_t[m], (1, 1)).astype(jnp.bfloat16)
        copy = pltpu.make_async_copy(
            turned.at[m], (gate_ref, up_ref, down_ref)[kind].at[head], sems.at[m]
        )
        copy.start()
        copies.append(copy)
    for copy in copies:
        copy.wait()


def solution(mesh):
    def step(queries, keys, values, rates, gate_fast, down_fast, up_fast):
        size = {"x": NX, "z": NZ}
        bf16 = jnp.bfloat16

        def per_group(shape):
            return [
                pltpu.VMEM(shape(1 if paired else count, axis), bf16)
                for _, count, axis, paired in GROUPS
            ]

        slab = lambda axis: WIDTH // size[axis]
        rest = lambda axis: NX * NZ // size[axis]
        vmem = pl.BlockSpec(memory_space=pltpu.VMEM)
        anywhere = pl.BlockSpec(memory_space=pltpu.HBM)
        groups = len(GROUPS)
        weight = gate_fast.shape
        outs = (
            jax.ShapeDtypeStruct(queries.shape, bf16),
            jax.ShapeDtypeStruct(weight, bf16),
            jax.ShapeDtypeStruct(weight, bf16),
            jax.ShapeDtypeStruct(weight, bf16),
        )
        staged, next_t = pl.pallas_call(
            kernel,
            out_shape=(
                pltpu.VMEM(queries.shape, bf16),
                pltpu.VMEM((MATS, WIDTH, WIDTH), bf16),
            ),
            in_specs=[anywhere] * 7,
            out_specs=[vmem] * 2,
            scratch_shapes=[
                pltpu.VMEM((ROWS, 8 * WIDTH), bf16),
                pltpu.VMEM((8, ROWS), jnp.float32),
                pltpu.VMEM(weight, bf16),
                pltpu.VMEM(weight, bf16),
                pltpu.VMEM(weight, bf16),
                pltpu.VMEM((ROWS, 8 * WIDTH), bf16),
                pltpu.VMEM((4 * ROWS, PAIR), bf16),
                pltpu.VMEM((4 * ROWS, PAIR), bf16),
                pltpu.VMEM((4 * ROWS, PAIR), bf16),
                pltpu.VMEM((4 * ROWS, WIDTH), bf16),
                pltpu.VMEM((4 * ROWS, WIDTH), bf16),
                pltpu.VMEM((4 * ROWS, WIDTH), bf16),
                pltpu.VMEM((MATS, WIDTH, WIDTH), bf16),
                pltpu.VMEM((4 * ROWS, WIDTH), bf16),
                pltpu.VMEM((4 * ROWS, PAIR), bf16),
                per_group(lambda count, axis: (size[axis] - 1, count, slab(axis), WIDTH)),
                per_group(lambda count, axis: (count, slab(axis), WIDTH)),
                per_group(lambda count, axis: (rest(axis) - 1, count, PIECE, WIDTH)),
                per_group(lambda count, axis: (count, PIECE, WIDTH)),
                per_group(lambda count, axis: (count, PIECE, WIDTH)),
                pltpu.SemaphoreType.DMA((7,)),
                pltpu.SemaphoreType.DMA((3, 2, 3)),
                pltpu.SemaphoreType.DMA((3, 2, 3)),
                pltpu.SemaphoreType.DMA((groups, 2, NZ - 1)),
                pltpu.SemaphoreType.DMA((groups, 2, NZ - 1)),
                pltpu.SemaphoreType.DMA((groups,)),
                pltpu.SemaphoreType.DMA((groups,)),
                pltpu.SemaphoreType.DMA((groups, NZ - 1)),
                pltpu.SemaphoreType.DMA((groups, NZ - 1)),
                pltpu.SemaphoreType.DMA((groups, NZ - 1)),
                pltpu.SemaphoreType.DMA((groups, NZ - 1)),
                pltpu.SemaphoreType.DMA((2, 3)),
                pltpu.SemaphoreType.DMA((2, 3)),
                pltpu.VMEM((WIDTH, WIDTH), bf16),
                pltpu.VMEM((1, WIDTH, WIDTH), bf16),
                pltpu.SemaphoreType.DMA((2,)),
                pltpu.SemaphoreType.DMA((2,)),
            ],
            compiler_params=pltpu.CompilerParams(
                collective_id=0, has_side_effects=True, vmem_limit_bytes=40 << 20
            ),
        )(
            *(
                pltpu.with_memory_space_constraint(array, pltpu.HBM)
                for array in (queries, keys, values, rates.T, gate_fast, down_fast, up_fast)
            )
        )
        return pl.pallas_call(
            finish,
            out_shape=outs,
            in_specs=[vmem] * 2,
            out_specs=[anywhere] * 4,
            scratch_shapes=[
                pltpu.VMEM((MATS, WIDTH, WIDTH), bf16),
                pltpu.SemaphoreType.DMA((MATS + 1,)),
            ],
            compiler_params=pltpu.CompilerParams(vmem_limit_bytes=12 << 20),
        )(staged, next_t)

    tokens = P(("heads", "tokens"), None)
    weights = P("heads", None, None)
    return jax.shard_map(
        step,
        mesh=mesh,
        in_specs=(tokens,) * 4 + (weights,) * 3,
        out_specs=(tokens,) + (weights,) * 3,
        check_vma=False,
    )
```

```python
import functools

import jax
import jax.numpy as jnp
from jax import lax
from jax.experimental import pallas as pl
from jax.experimental.pallas import tpu as pltpu
from jax.sharding import PartitionSpec as P

MESH = pl.DeviceIdType.MESH
NX, NZ = 4, 8
ROWS = 128
WIDTH = 512
PAIR = 2 * WIDTH
MATS = 6
PIECE = WIDTH // (NX * NZ)

GROUPS = ((0, 2, "x", False), (2, 1, "z", False), (3, 2, "x", True), (5, 1, "x", False))
PAIRED = 2
CHUNKS = (1, 1, 2, 2)
FAR = {1: (0,), 2: (1, 0), 4: (2, 1, 3, 0), 8: (4, 3, 5, 2, 6, 1, 7, 0)}


def dot(left, right, dims):
    return lax.dot_general(
        left, right, ((dims[:1], dims[1:]), ((), ())), preferred_element_type=jnp.float32
    )


def kernel(
    q_hbm, k_hbm, v_hbm, rate_hbm, gate_hbm, down_hbm, up_hbm,
    out_ref, turned,
    v_ref, rate_ref, gate_ref, down_ref, up_ref,
    d_own, k_all, d_all, q_all, hid, d_gate, d_up, grads, mixed, results, next_t,
    first_in, first_sum, second_in, second_sum, last_in,
    local_sem, in_send, in_recv, slab_send, slab_recv, red_send, red_recv, last_send, last_recv,
    gat_send, gat_recv, for_send, for_recv, out_send, out_recv,
    pair_in, pair_sum, pair_send, pair_recv,
):
    group = lax.axis_index("heads")
    place = lax.axis_index("tokens")
    y_lo, core = group // 2, group % 2
    x, z, y_hi = place // 16, (place // 2) % 8, place % 2
    y = y_hi * 2 + y_lo

    def device(y, core, x, z):
        return ((y % 2) * 2 + core, (x * NZ + z) * 2 + y // 2)

    peers = {
        "x": [device(y, core, (x + step) % NX, z) for step in range(1, NX)],
        "z": [device(y, core, x, (z + step) % NZ) for step in range(1, NZ)],
    }
    position = {"x": x, "z": z}
    size = {"x": NX, "z": NZ}
    other = {"x": "z", "z": "x"}
    opposite = device((y + 2) % 4, core, x, z)
    sibling = device(y, 1 - core, x, z)
    forward = (y + 1 + 2 * core) % 4
    targets = [sibling, device(forward, 0, x, z), device(forward, 1, x, z)]
    below, above = device((y + 3) % 4, 0, x, z), device((y + 1) % 4, 1, x, z)
    sources = [sibling, below, above]
    target_group = [y_lo * 2 + 1 - core, (1 - y_lo) * 2, (1 - y_lo) * 2 + 1]
    target_slot = [1, 2 + core, 2 + core]
    source_group = [y_lo * 2 + 1 - core, (1 - y_lo) * 2, (1 - y_lo) * 2 + 1]

    barrier = pltpu.get_barrier_semaphore()
    greeted = peers["x"] + peers["z"] + [opposite] + targets + sources[1:]
    for peer in greeted:
        pl.semaphore_signal(barrier, inc=1, device_id=peer, device_id_type=MESH)

    def columns(of_group, head):
        return pl.ds(pl.multiple_of(of_group * PAIR, PAIR) + head * WIDTH, WIDTH)

    def slot_rows(slot):
        if isinstance(slot, int):
            return pl.ds(slot * ROWS, ROWS)
        return pl.ds(pl.multiple_of(slot * ROWS, ROWS), ROWS)

    started = []

    def send(src, dst, send_sem, recv_sem, to):
        copy = pltpu.make_async_remote_copy(
            src_ref=src, dst_ref=dst, send_sem=send_sem, recv_sem=recv_sem,
            device_id=to, device_id_type=MESH,
        )
        copy.start()
        started.append(copy)
        return copy

    incoming = {}

    def local(src, dst, index):
        copy = pltpu.make_async_copy(src, dst, local_sem.at[index])
        copy.start()
        return copy

    own_cols = pl.ds(pl.multiple_of(group * PAIR, PAIR), PAIR)
    loads = {
        name: local(src, dst, index)
        for index, (name, src, dst) in enumerate(
            (
                ("rate", rate_hbm, rate_ref),
                ("value", v_hbm, v_ref),
                ("key", k_hbm.at[:, own_cols], k_all.at[slot_rows(0), :]),
                ("gate", gate_hbm, gate_ref),
                ("up", up_hbm, up_ref),
                ("down", down_hbm, down_ref),
                ("query", q_hbm.at[:, own_cols], q_all.at[slot_rows(0), :]),
            )
        )
    }

    loads["rate"].wait()
    rate_cols = jnp.transpose(rate_ref[...])
    loads["value"].wait()
    for head in range(8):
        cols = slice(head * WIDTH, (head + 1) * WIDTH)
        d_own[:, cols] = (-rate_cols[:, head : head + 1] * v_ref[:, cols].astype(jnp.float32)).astype(
            jnp.bfloat16
        )

    pl.semaphore_wait(barrier, len(greeted))

    def exchange(which, src, dst, head):
        for n in (1, 2, 0):
            index = 0 if n == 0 else 1 + core
            send(
                src.at[:, columns(target_group[n], head)],
                dst.at[slot_rows(target_slot[n]), pl.ds(head * WIDTH, WIDTH)],
                in_send.at[which, head, n], in_recv.at[which, head, index], targets[n],
            )

    def arrived(which, dst, head, n):
        there = dst.at[slot_rows(1 + n), pl.ds(head * WIDTH, WIDTH)]
        pltpu.make_async_remote_copy(
            src_ref=there, dst_ref=there, send_sem=in_send.at[which, head, n],
            recv_sem=in_recv.at[which, head, n], device_id=sources[n], device_id_type=MESH,
        ).wait_recv()

    for head in range(2):
        exchange(0, k_hbm, k_all, head)
        exchange(1, d_own, d_all, head)
    d_all[slot_rows(0), :] = d_own[:, own_cols]
    for name in ("key", "gate", "up", "down"):
        loads[name].wait()

    def gradients(head):
        cols = slice(head * WIDTH, (head + 1) * WIDTH)
        for half in range(2):
            if half == 0:
                arrived(0, k_all, head, 0)
                arrived(1, d_all, head, 0)
            else:
                for n in (1, 2):
                    arrived(0, k_all, head, n)
                    arrived(1, d_all, head, n)
            rows = slice(half * 2 * ROWS, (half + 1) * 2 * ROWS)
            keys = k_all[rows, cols]
            d_out = d_all[rows, cols]
            gate_pre = dot(keys, gate_ref[head], (1, 0))
            up_pre = dot(keys, up_ref[head], (1, 0))
            d_hidden = dot(d_out, down_ref[head], (1, 1))
            sigma = jax.nn.sigmoid(gate_pre)
            silu = gate_pre * sigma
            hid[rows, :] = (silu * up_pre).astype(jnp.bfloat16)
            d_gate[rows, :] = (d_hidden * up_pre * sigma * (1.0 + gate_pre * (1.0 - sigma))).astype(
                jnp.bfloat16
            )
            d_up[rows, :] = (d_hidden * silu).astype(jnp.bfloat16)
        base = 3 * head
        if head == 0:
            grads[base + 2] = dot(d_all[:, cols], hid[...], (0, 0)).astype(jnp.bfloat16)
            reduce_start(1)
        grads[base] = dot(d_gate[...], k_all[:, cols], (0, 0)).astype(jnp.bfloat16)
        grads[base + 1] = dot(d_up[...], k_all[:, cols], (0, 0)).astype(jnp.bfloat16)
        if head == 0:
            reduce_start(0)
        else:
            pair_start()
            grads[base + 2] = dot(d_all[:, cols], hid[...], (0, 0)).astype(jnp.bfloat16)
            reduce_start(3)

    def slab(axis, index, rows):
        return pl.ds(pl.multiple_of(index * rows, rows), rows)

    def matrices(g):
        first, count, _, paired = GROUPS[g]
        return pl.ds(first + y_hi, 1) if paired else pl.ds(first, count)

    def at_rows(start, rows):
        return pl.ds(pl.multiple_of(start, PIECE), rows)

    def chunk(g, k):
        axis = GROUPS[g][2]
        far, chunks = other[axis], CHUNKS[g]
        owners = size[far] // chunks
        index = (position[far] // owners + k) % chunks
        return index * owners * PIECE, owners * PIECE, index * owners

    def pair_copy(k, part):
        start, rows, _ = chunk(PAIRED, k)
        here = at_rows(part * (WIDTH // NX) + start, rows)
        return pltpu.make_async_remote_copy(
            src_ref=grads.at[GROUPS[PAIRED][0] + 1 - y_hi, here, :], dst_ref=pair_in.at[here, :],
            send_sem=pair_send.at[0], recv_sem=pair_recv.at[1 + k],
            device_id=opposite, device_id_type=MESH,
        )

    def pair_start():
        for k in FAR[CHUNKS[PAIRED]]:
            for part in range(NX):
                pair_copy(k, part).start()

    def pair_chunk(k):
        start, rows, _ = chunk(PAIRED, k)
        four = pair_in.at[pl.ds(0, NX * rows), :]
        pltpu.make_async_remote_copy(
            src_ref=four, dst_ref=four, send_sem=pair_send.at[0], recv_sem=pair_recv.at[1 + k],
            device_id=opposite, device_id_type=MESH,
        ).wait_recv()
        for part in range(NX):
            here = at_rows(part * (WIDTH // NX) + start, rows)
            pair_sum[0, here, :] = (
                grads[GROUPS[PAIRED][0] + y_hi, here, :].astype(jnp.float32)
                + pair_in[here, :].astype(jnp.float32)
            ).astype(jnp.bfloat16)
        reduce_chunk_start(PAIRED, k)

    def slab_copy(g, k, n):
        axis = GROUPS[g][2]
        start, rows, _ = chunk(g, k)
        src = pair_sum if GROUPS[g][3] else grads.at[matrices(g)]
        target = (position[axis] + n + 1) % size[axis]
        return pltpu.make_async_remote_copy(
            src_ref=src.at[:, at_rows(target * (WIDTH // size[axis]) + start, rows), :],
            dst_ref=first_in[g].at[n, :, at_rows(start, rows), :],
            send_sem=slab_send.at[g, n], recv_sem=slab_recv.at[g, k, n],
            device_id=peers[axis][n], device_id_type=MESH,
        )

    def reduce_chunk_start(g, k):
        for n in range(len(peers[GROUPS[g][2]])):
            slab_copy(g, k, n).start()

    def reduce_start(g):
        for k in FAR[CHUNKS[g]]:
            reduce_chunk_start(g, k)

    def owner(axis, index):
        return device(y, core, index, z) if axis == "x" else device(y, core, x, index)

    def reduce_chunk(g, k):
        axis = GROUPS[g][2]
        far = other[axis]
        start, rows, begin = chunk(g, k)
        src = pair_sum if GROUPS[g][3] else grads.at[matrices(g)]
        for n in range(len(peers[axis])):
            slab_copy(g, k, n).wait_recv()
        here = at_rows(start, rows)
        mine = at_rows(position[axis] * (WIDTH // size[axis]) + start, rows)
        for m in range(first_sum[g].shape[0]):
            own = src[m, mine, :].astype(jnp.float32)
            for n in range(len(peers[axis])):
                own = own + first_in[g][n, m, here, :].astype(jnp.float32)
            first_sum[g][m, here, :] = own.astype(jnp.bfloat16)
        owners = size[far] // CHUNKS[g]
        for d in range(owners):
            if k == 0 and d == 0:
                continue
            index = begin + (position[far] + d) % owners
            slot = k * owners + d - 1
            incoming["reduce", g, slot] = send(
                first_sum[g].at[:, at_rows(index * PIECE, PIECE), :], second_in[g].at[slot],
                red_send.at[g, slot], red_recv.at[g, slot], owner(far, index),
            )

    def reduce_sent(g):
        axis = GROUPS[g][2]
        for n in range(len(peers[axis])):
            slab = first_in[g].at[n]
            pltpu.make_async_remote_copy(
                src_ref=slab, dst_ref=slab, send_sem=slab_send.at[g, n],
                recv_sem=slab_recv.at[g, 0, n], device_id=peers[axis][n], device_id_type=MESH,
            ).wait_send()

    def reduce_finish(g):
        far = other[GROUPS[g][2]]
        for n in range(len(peers[far])):
            incoming["reduce", g, n].wait_recv()
        for m in range(second_sum[g].shape[0]):
            own = first_sum[g][m, at_rows(position[far] * PIECE, PIECE), :].astype(jnp.float32)
            for n in range(len(peers[far])):
                own = own + second_in[g][n, m].astype(jnp.float32)
            second_sum[g][m] = own.astype(jnp.bfloat16)

    def last_start(g):
        incoming["last", g] = send(
            second_sum[g], last_in[g], last_send.at[g], last_recv.at[g], opposite
        )

    def renormed(g):
        first, count, axis, paired = GROUPS[g]
        begin = position[axis] * (WIDTH // size[axis]) + position[other[axis]] * PIECE
        chosen = (
            lax.broadcasted_iota(jnp.int32, (PIECE, WIDTH), 1)
            == lax.broadcasted_iota(jnp.int32, (PIECE, WIDTH), 0) + begin
        )
        pick = jnp.where(chosen, 1.0, 0.0).astype(jnp.bfloat16)

        def old(m):
            head, kind = divmod(m, 3)
            return dot(pick, (gate_ref, up_ref, down_ref)[kind][head], (1, 1))

        if not paired:
            incoming["last", g].wait_recv()
        for m in range(1 if paired else count):
            total = second_sum[g][m].astype(jnp.float32)
            if paired:
                wide = jnp.where(y_hi == 0, old(first), old(first + 1))
            else:
                wide = old(first + m)
                total = total + last_in[g][m].astype(jnp.float32)
            moved = wide - total
            factor = jnp.sqrt(jnp.sum(wide * wide, axis=1, keepdims=True)) / jnp.sqrt(
                jnp.sum(moved * moved, axis=1, keepdims=True) + 1e-06
            )
            index = first + y_hi if paired else first + m
            next_t[index, pl.ds(pl.multiple_of(begin, PIECE), PIECE), :] = (moved * factor).astype(
                jnp.bfloat16
            )

    def piece(g, index):
        axis = GROUPS[g][2]
        begin = position[axis] * (WIDTH // size[axis]) + index * PIECE
        return next_t.at[matrices(g), pl.ds(pl.multiple_of(begin, PIECE), PIECE), :]

    def forward_piece(g, index):
        for n, peer in enumerate(peers[GROUPS[g][2]]):
            pltpu.make_async_remote_copy(
                src_ref=piece(g, index), dst_ref=piece(g, index),
                send_sem=for_send.at[g, n], recv_sem=for_recv.at[g, n],
                device_id=peer, device_id_type=MESH,
            ).start()

    def gather_start(g):
        axis = other[GROUPS[g][2]]
        here = piece(g, position[axis])
        for n, peer in enumerate(peers[axis]):
            incoming["gather", g, n] = send(here, here, gat_send.at[g, n], gat_recv.at[g, n], peer)
        forward_piece(g, position[axis])

    def gather_forward(g):
        axis = other[GROUPS[g][2]]
        for n in range(len(peers[axis])):
            incoming["gather", g, n].wait_recv()
            forward_piece(g, (position[axis] + size[axis] - n - 1) % size[axis])

    def whole_slab(g, n):
        axis = GROUPS[g][2]
        here = next_t.at[matrices(g), slab(axis, position[axis], WIDTH // size[axis]), :]
        return pltpu.make_async_remote_copy(
            src_ref=here, dst_ref=here, send_sem=for_send.at[g, n], recv_sem=for_recv.at[g, n],
            device_id=peers[axis][n], device_id_type=MESH,
        )

    def gather_finish(g):
        for n in range(len(peers[GROUPS[g][2]])):
            whole_slab(g, n).wait_recv()

    def share_slab(index):
        here = next_t.at[matrices(PAIRED), slab("x", index, WIDTH // NX), :]
        pltpu.make_async_remote_copy(
            src_ref=here, dst_ref=here, send_sem=pair_send.at[1], recv_sem=pair_recv.at[0],
            device_id=opposite, device_id_type=MESH,
        ).start()

    def share():
        share_slab(x)
        for n in range(NX - 1):
            whole_slab(PAIRED, n).wait_recv()
            share_slab((x + NX - n - 1) % NX)

    def shared():
        here = next_t.at[matrices(PAIRED)]
        return pltpu.make_async_remote_copy(
            src_ref=here, dst_ref=here, send_sem=pair_send.at[1], recv_sem=pair_recv.at[0],
            device_id=opposite, device_id_type=MESH,
        )

    for head in range(2):
        gradients(head)
    for head in range(2):
        exchange(2, q_hbm, q_all, head)
    for g in (0, 1):
        for k in FAR[CHUNKS[g]]:
            reduce_chunk(g, k)
    order = FAR[CHUNKS[PAIRED]]
    for k in order:
        pair_chunk(k)
        reduce_chunk(3, k)
    for g in (0, 1):
        reduce_finish(g)
        last_start(g)
    for k in order:
        reduce_chunk(PAIRED, k)
    reduce_finish(3)
    last_start(3)
    for g in (0, 1, 3):
        renormed(g)
        gather_start(g)
    reduce_finish(PAIRED)
    renormed(PAIRED)
    gather_start(PAIRED)
    for g in (0, 1, 3, PAIRED):
        gather_forward(g)
    share()
    loads["query"].wait()

    same = (
        lax.broadcasted_iota(jnp.int32, (WIDTH, WIDTH), 0)
        == lax.broadcasted_iota(jnp.int32, (WIDTH, WIDTH), 1)
    )
    unit = jnp.where(same, 1.0, 0.0).astype(jnp.bfloat16)
    for head in range(2):
        cols = slice(head * WIDTH, (head + 1) * WIDTH)
        for n in range(3):
            arrived(2, q_all, head, n)
        if head == 0:
            gather_finish(0)
            gather_finish(1)
        else:
            gather_finish(3)
            shared().wait_recv()
        for half in (1, 0):
            rows = slice(half * 2 * ROWS, (half + 1) * 2 * ROWS)
            queries = q_all[rows, cols]
            first = dot(queries, next_t[3 * head], (1, 1))
            second = dot(queries, next_t[3 * head + 1], (1, 1))
            mixed[rows, :] = (first * jax.nn.sigmoid(first) * second).astype(jnp.bfloat16)
            results[rows, cols] = dot(mixed[rows, :], next_t[3 * head + 2], (1, 1)).astype(
                jnp.bfloat16
            )
            for n in ((1, 2) if half else (0,)):
                index = 0 if n == 0 else 1 + core
                send(
                    results.at[slot_rows(1 + n), cols], out_ref.at[:, columns(group, head)],
                    out_send.at[head, n], out_recv.at[head, index], sources[n],
                )
        out_ref[:, columns(group, head)] = results[slot_rows(0), cols]
    for m in range(MATS):
        turned[m] = dot(unit, next_t[m], (1, 1)).astype(jnp.bfloat16)

    for head in range(2):
        for n in range(3):
            there = out_ref.at[:, columns(target_group[n], head)]
            pltpu.make_async_remote_copy(
                src_ref=there, dst_ref=there, send_sem=out_send.at[head, n],
                recv_sem=out_recv.at[head, n], device_id=targets[n], device_id_type=MESH,
            ).wait_recv()
    for copy in started:
        copy.wait_send()
    shared().wait_send()
    pltpu.make_async_remote_copy(
        src_ref=pair_in, dst_ref=pair_in, send_sem=pair_send.at[0], recv_sem=pair_recv.at[0],
        device_id=opposite, device_id_type=MESH,
    ).wait_send()
    for g in range(len(GROUPS)):
        reduce_sent(g)
        for n in range(len(peers[GROUPS[g][2]])):
            whole_slab(g, n).wait_send()


def finish(staged, turned, out_ref, gate_ref, down_ref, up_ref, sems):
    copies = [pltpu.make_async_copy(staged, out_ref, sems.at[MATS])]
    for m in range(MATS):
        head, kind = divmod(m, 3)
        copies.append(
            pltpu.make_async_copy(
                turned.at[m], (gate_ref, up_ref, down_ref)[kind].at[head], sems.at[m]
            )
        )
    for copy in copies:
        copy.start()
    for copy in copies:
        copy.wait()


def solution(mesh):
    def step(queries, keys, values, rates, gate_fast, down_fast, up_fast):
        size = {"x": NX, "z": NZ}
        bf16 = jnp.bfloat16

        def per_group(shape):
            return [
                pltpu.VMEM(shape(1 if paired else count, axis), bf16)
                for _, count, axis, paired in GROUPS
            ]

        slab = lambda axis: WIDTH // size[axis]
        rest = lambda axis: NX * NZ // size[axis]
        vmem = pl.BlockSpec(memory_space=pltpu.VMEM)
        anywhere = pl.BlockSpec(memory_space=pltpu.HBM)
        groups = len(GROUPS)
        weight = gate_fast.shape
        outs = (
            jax.ShapeDtypeStruct(queries.shape, bf16),
            jax.ShapeDtypeStruct(weight, bf16),
            jax.ShapeDtypeStruct(weight, bf16),
            jax.ShapeDtypeStruct(weight, bf16),
        )
        staged, turned = pl.pallas_call(
            kernel,
            out_shape=(
                pltpu.VMEM(queries.shape, bf16),
                pltpu.VMEM((MATS, WIDTH, WIDTH), bf16),
            ),
            in_specs=[anywhere] * 7,
            out_specs=[vmem] * 2,
            scratch_shapes=[
                pltpu.VMEM((ROWS, 8 * WIDTH), bf16),
                pltpu.VMEM((8, ROWS), jnp.float32),
                pltpu.VMEM(weight, bf16),
                pltpu.VMEM(weight, bf16),
                pltpu.VMEM(weight, bf16),
                pltpu.VMEM((ROWS, 8 * WIDTH), bf16),
                pltpu.VMEM((4 * ROWS, PAIR), bf16),
                pltpu.VMEM((4 * ROWS, PAIR), bf16),
                pltpu.VMEM((4 * ROWS, PAIR), bf16),
                pltpu.VMEM((4 * ROWS, WIDTH), bf16),
                pltpu.VMEM((4 * ROWS, WIDTH), bf16),
                pltpu.VMEM((4 * ROWS, WIDTH), bf16),
                pltpu.VMEM((MATS, WIDTH, WIDTH), bf16),
                pltpu.VMEM((4 * ROWS, WIDTH), bf16),
                pltpu.VMEM((4 * ROWS, PAIR), bf16),
                pltpu.VMEM((MATS, WIDTH, WIDTH), bf16),
                per_group(lambda count, axis: (size[axis] - 1, count, slab(axis), WIDTH)),
                per_group(lambda count, axis: (count, slab(axis), WIDTH)),
                per_group(lambda count, axis: (rest(axis) - 1, count, PIECE, WIDTH)),
                per_group(lambda count, axis: (count, PIECE, WIDTH)),
                per_group(lambda count, axis: (count, PIECE, WIDTH)),
                pltpu.SemaphoreType.DMA((7,)),
                pltpu.SemaphoreType.DMA((3, 2, 3)),
                pltpu.SemaphoreType.DMA((3, 2, 3)),
                pltpu.SemaphoreType.DMA((groups, NZ - 1)),
                pltpu.SemaphoreType.DMA((groups, NZ, NZ - 1)),
                pltpu.SemaphoreType.DMA((groups, NZ - 1)),
                pltpu.SemaphoreType.DMA((groups, NZ - 1)),
                pltpu.SemaphoreType.DMA((groups,)),
                pltpu.SemaphoreType.DMA((groups,)),
                pltpu.SemaphoreType.DMA((groups, NZ - 1)),
                pltpu.SemaphoreType.DMA((groups, NZ - 1)),
                pltpu.SemaphoreType.DMA((groups, NZ - 1)),
                pltpu.SemaphoreType.DMA((groups, NZ - 1)),
                pltpu.SemaphoreType.DMA((2, 3)),
                pltpu.SemaphoreType.DMA((2, 3)),
                pltpu.VMEM((WIDTH, WIDTH), bf16),
                pltpu.VMEM((1, WIDTH, WIDTH), bf16),
                pltpu.SemaphoreType.DMA((2,)),
                pltpu.SemaphoreType.DMA((1 + NZ,)),
            ],
            compiler_params=pltpu.CompilerParams(
                collective_id=0, has_side_effects=True, vmem_limit_bytes=40 << 20
            ),
        )(
            *(
                pltpu.with_memory_space_constraint(array, pltpu.HBM)
                for array in (queries, keys, values, rates.T, gate_fast, down_fast, up_fast)
            )
        )
        return pl.pallas_call(
            finish,
            out_shape=outs,
            in_specs=[vmem] * 2,
            out_specs=[anywhere] * 4,
            scratch_shapes=[pltpu.SemaphoreType.DMA((MATS + 1,))],
            compiler_params=pltpu.CompilerParams(vmem_limit_bytes=12 << 20),
        )(staged, turned)

    tokens = P(("heads", "tokens"), None)
    weights = P("heads", None, None)
    return jax.shard_map(
        step,
        mesh=mesh,
        in_specs=(tokens,) * 4 + (weights,) * 3,
        out_specs=(tokens,) + (weights,) * 3,
        check_vma=False,
    )
```

```python
import functools

import jax
import jax.numpy as jnp
from jax import lax
from jax.experimental import pallas as pl
from jax.experimental.pallas import tpu as pltpu
from jax.sharding import PartitionSpec as P

MESH = pl.DeviceIdType.MESH
NX, NZ = 4, 8
ROWS = 128
WIDTH = 512
PAIR = 2 * WIDTH
MATS = 6
PIECE = WIDTH // (NX * NZ)

GROUPS = ((0, 2, "x", False), (2, 1, "z", False), (3, 2, "x", True), (5, 1, "x", False))
PAIRED = 2


def dot(left, right, dims):
    return lax.dot_general(
        left, right, ((dims[:1], dims[1:]), ((), ())), preferred_element_type=jnp.float32
    )


def kernel(
    q_hbm, k_hbm, v_hbm, rate_hbm, gate_hbm, down_hbm, up_hbm,
    out_ref, next_t,
    v_ref, rate_ref, gate_ref, down_ref, up_ref,
    d_own, k_all, d_all, q_all, hid, d_gate, d_up, grads, mixed, results,
    first_in, first_sum, second_in, second_sum, last_in,
    local_sem, in_send, in_recv, red_send, red_recv, last_send, last_recv,
    gat_send, gat_recv, for_send, for_recv, out_send, out_recv,
    pair_in, pair_sum, pair_send, pair_recv,
):
    group = lax.axis_index("heads")
    place = lax.axis_index("tokens")
    y_lo, core = group // 2, group % 2
    x, z, y_hi = place // 16, (place // 2) % 8, place % 2
    y = y_hi * 2 + y_lo

    def device(y, core, x, z):
        return ((y % 2) * 2 + core, (x * NZ + z) * 2 + y // 2)

    peers = {
        "x": [device(y, core, (x + step) % NX, z) for step in range(1, NX)],
        "z": [device(y, core, x, (z + step) % NZ) for step in range(1, NZ)],
    }
    position = {"x": x, "z": z}
    size = {"x": NX, "z": NZ}
    other = {"x": "z", "z": "x"}
    opposite = device((y + 2) % 4, core, x, z)
    sibling = device(y, 1 - core, x, z)
    forward = (y + 1 + 2 * core) % 4
    targets = [sibling, device(forward, 0, x, z), device(forward, 1, x, z)]
    below, above = device((y + 3) % 4, 0, x, z), device((y + 1) % 4, 1, x, z)
    sources = [sibling, below, above]
    target_group = [y_lo * 2 + 1 - core, (1 - y_lo) * 2, (1 - y_lo) * 2 + 1]
    target_slot = [1, 2 + core, 2 + core]
    source_group = [y_lo * 2 + 1 - core, (1 - y_lo) * 2, (1 - y_lo) * 2 + 1]

    barrier = pltpu.get_barrier_semaphore()
    greeted = peers["x"] + peers["z"] + [opposite] + targets + sources[1:]
    for peer in greeted:
        pl.semaphore_signal(barrier, inc=1, device_id=peer, device_id_type=MESH)

    def columns(of_group, head):
        return pl.ds(pl.multiple_of(of_group * PAIR, PAIR) + head * WIDTH, WIDTH)

    def slot_rows(slot):
        if isinstance(slot, int):
            return pl.ds(slot * ROWS, ROWS)
        return pl.ds(pl.multiple_of(slot * ROWS, ROWS), ROWS)

    started = []

    def send(src, dst, send_sem, recv_sem, to):
        copy = pltpu.make_async_remote_copy(
            src_ref=src, dst_ref=dst, send_sem=send_sem, recv_sem=recv_sem,
            device_id=to, device_id_type=MESH,
        )
        copy.start()
        started.append(copy)
        return copy

    incoming = {}

    def local(src, dst, index):
        copy = pltpu.make_async_copy(src, dst, local_sem.at[index])
        copy.start()
        return copy

    own_cols = pl.ds(pl.multiple_of(group * PAIR, PAIR), PAIR)
    loads = {
        name: local(src, dst, index)
        for index, (name, src, dst) in enumerate(
            (
                ("rate", rate_hbm, rate_ref),
                ("value", v_hbm, v_ref),
                ("key", k_hbm.at[:, own_cols], k_all.at[slot_rows(0), :]),
                ("gate", gate_hbm, gate_ref),
                ("up", up_hbm, up_ref),
                ("down", down_hbm, down_ref),
                ("query", q_hbm.at[:, own_cols], q_all.at[slot_rows(0), :]),
            )
        )
    }

    pl.semaphore_wait(barrier, len(greeted))

    def exchange(which, src, dst, head):
        for n in (1, 2, 0):
            index = 0 if n == 0 else 1 + core
            send(
                src.at[:, columns(target_group[n], head)],
                dst.at[slot_rows(target_slot[n]), pl.ds(head * WIDTH, WIDTH)],
                in_send.at[which, head, n], in_recv.at[which, head, index], targets[n],
            )

    def arrived(which, dst, head, n):
        there = dst.at[slot_rows(1 + n), pl.ds(head * WIDTH, WIDTH)]
        pltpu.make_async_remote_copy(
            src_ref=there, dst_ref=there, send_sem=in_send.at[which, head, n],
            recv_sem=in_recv.at[which, head, n], device_id=sources[n], device_id_type=MESH,
        ).wait_recv()

    exchange(0, k_hbm, k_all, 0)
    loads["rate"].wait()
    rate_cols = jnp.transpose(rate_ref[...])
    loads["value"].wait()
    for head in range(2):
        for of_group in range(4):
            index = 2 * of_group + head
            cols = slice(index * WIDTH, (index + 1) * WIDTH)
            d_own[:, cols] = (
                -rate_cols[:, index : index + 1] * v_ref[:, cols].astype(jnp.float32)
            ).astype(jnp.bfloat16)
        exchange(1, d_own, d_all, head)
        if head == 0:
            exchange(0, k_hbm, k_all, 1)
    d_all[slot_rows(0), :] = d_own[:, own_cols]
    for name in ("key", "gate", "up", "down"):
        loads[name].wait()

    def gradients(head):
        cols = slice(head * WIDTH, (head + 1) * WIDTH)
        for half in range(2):
            if half == 0:
                arrived(0, k_all, head, 0)
                arrived(1, d_all, head, 0)
            else:
                for n in (1, 2):
                    arrived(0, k_all, head, n)
                    arrived(1, d_all, head, n)
            rows = slice(half * 2 * ROWS, (half + 1) * 2 * ROWS)
            keys = k_all[rows, cols]
            d_out = d_all[rows, cols]
            gate_pre = dot(keys, gate_ref[head], (1, 0))
            up_pre = dot(keys, up_ref[head], (1, 0))
            d_hidden = dot(d_out, down_ref[head], (1, 1))
            sigma = jax.nn.sigmoid(gate_pre)
            silu = gate_pre * sigma
            hid[rows, :] = (silu * up_pre).astype(jnp.bfloat16)
            d_gate[rows, :] = (d_hidden * up_pre * sigma * (1.0 + gate_pre * (1.0 - sigma))).astype(
                jnp.bfloat16
            )
            d_up[rows, :] = (d_hidden * silu).astype(jnp.bfloat16)
        base = 3 * head
        if head == 0:
            grads[base + 2] = dot(d_all[:, cols], hid[...], (0, 0)).astype(jnp.bfloat16)
            reduce_start(1, 0)
        grads[base] = dot(d_gate[...], k_all[:, cols], (0, 0)).astype(jnp.bfloat16)
        grads[base + 1] = dot(d_up[...], k_all[:, cols], (0, 0)).astype(jnp.bfloat16)
        if head == 0:
            reduce_start(0, 0)
        else:
            pair_start()
            grads[base + 2] = dot(d_all[:, cols], hid[...], (0, 0)).astype(jnp.bfloat16)
            reduce_start(3, 0)

    def slab(axis, index, rows):
        return pl.ds(pl.multiple_of(index * rows, rows), rows)

    def matrices(g):
        first, count, _, paired = GROUPS[g]
        return pl.ds(first + y_hi, 1) if paired else pl.ds(first, count)

    def pair_start():
        first = GROUPS[PAIRED][0]
        incoming["pair"] = send(
            grads.at[first + 1 - y_hi], pair_in, pair_send.at[0], pair_recv.at[0], opposite
        )

    def pair_finish():
        first = GROUPS[PAIRED][0]
        incoming["pair"].wait_recv()
        pair_sum[0] = (
            grads[first + y_hi].astype(jnp.float32) + pair_in[...].astype(jnp.float32)
        ).astype(jnp.bfloat16)

    def reduce_buffers(g, level):
        _, count, axis, paired = GROUPS[g]
        if level == 0:
            src = pair_sum if paired else grads.at[matrices(g)]
            return src, first_in[g], first_sum[g], axis, WIDTH // size[axis]
        return first_sum[g], second_in[g], second_sum[g], other[axis], PIECE

    def reduce_start(g, level):
        src, dst, _, axis, rows = reduce_buffers(g, level)
        for n, peer in enumerate(peers[axis]):
            index = (position[axis] + n + 1) % size[axis]
            incoming["reduce", g, level, n] = send(
                src.at[:, slab(axis, index, rows), :], dst.at[n],
                red_send.at[g, level, n], red_recv.at[g, level, n], peer,
            )

    def reduce_finish(g, level):
        src, dst, total, axis, rows = reduce_buffers(g, level)
        for n in range(len(peers[axis])):
            incoming["reduce", g, level, n].wait_recv()
        for m in range(total.shape[0]):
            own = src[m, slab(axis, position[axis], rows), :].astype(jnp.float32)
            for n in range(len(peers[axis])):
                own = own + dst[n, m].astype(jnp.float32)
            total[m] = own.astype(jnp.bfloat16)

    def last_start(g):
        incoming["last", g] = send(
            second_sum[g], last_in[g], last_send.at[g], last_recv.at[g], opposite
        )

    def renormed(g):
        first, count, axis, paired = GROUPS[g]
        begin = position[axis] * (WIDTH // size[axis]) + position[other[axis]] * PIECE
        chosen = (
            lax.broadcasted_iota(jnp.int32, (PIECE, WIDTH), 1)
            == lax.broadcasted_iota(jnp.int32, (PIECE, WIDTH), 0) + begin
        )
        pick = jnp.where(chosen, 1.0, 0.0).astype(jnp.bfloat16)

        def old(m):
            head, kind = divmod(m, 3)
            return dot(pick, (gate_ref, up_ref, down_ref)[kind][head], (1, 1))

        if not paired:
            incoming["last", g].wait_recv()
        for m in range(1 if paired else count):
            total = second_sum[g][m].astype(jnp.float32)
            if paired:
                wide = jnp.where(y_hi == 0, old(first), old(first + 1))
            else:
                wide = old(first + m)
                total = total + last_in[g][m].astype(jnp.float32)
            moved = wide - total
            factor = jnp.sqrt(jnp.sum(wide * wide, axis=1, keepdims=True)) / jnp.sqrt(
                jnp.sum(moved * moved, axis=1, keepdims=True) + 1e-06
            )
            index = first + y_hi if paired else first + m
            next_t[index, pl.ds(pl.multiple_of(begin, PIECE), PIECE), :] = (moved * factor).astype(
                jnp.bfloat16
            )

    def piece(g, index):
        axis = GROUPS[g][2]
        begin = position[axis] * (WIDTH // size[axis]) + index * PIECE
        return next_t.at[matrices(g), pl.ds(pl.multiple_of(begin, PIECE), PIECE), :]

    def forward_piece(g, index):
        for n, peer in enumerate(peers[GROUPS[g][2]]):
            pltpu.make_async_remote_copy(
                src_ref=piece(g, index), dst_ref=piece(g, index),
                send_sem=for_send.at[g, n], recv_sem=for_recv.at[g, n],
                device_id=peer, device_id_type=MESH,
            ).start()

    def gather_start(g):
        axis = other[GROUPS[g][2]]
        here = piece(g, position[axis])
        for n, peer in enumerate(peers[axis]):
            incoming["gather", g, n] = send(here, here, gat_send.at[g, n], gat_recv.at[g, n], peer)
        forward_piece(g, position[axis])

    def gather_forward(g):
        axis = other[GROUPS[g][2]]
        for n in range(len(peers[axis])):
            incoming["gather", g, n].wait_recv()
            forward_piece(g, (position[axis] + size[axis] - n - 1) % size[axis])

    def whole_slab(g, n):
        axis = GROUPS[g][2]
        here = next_t.at[matrices(g), slab(axis, position[axis], WIDTH // size[axis]), :]
        return pltpu.make_async_remote_copy(
            src_ref=here, dst_ref=here, send_sem=for_send.at[g, n], recv_sem=for_recv.at[g, n],
            device_id=peers[axis][n], device_id_type=MESH,
        )

    def gather_finish(g):
        for n in range(len(peers[GROUPS[g][2]])):
            whole_slab(g, n).wait_recv()

    def share_slab(index):
        here = next_t.at[matrices(PAIRED), slab("x", index, WIDTH // NX), :]
        pltpu.make_async_remote_copy(
            src_ref=here, dst_ref=here, send_sem=pair_send.at[1], recv_sem=pair_recv.at[1],
            device_id=opposite, device_id_type=MESH,
        ).start()

    def share():
        share_slab(x)
        for n in range(NX - 1):
            whole_slab(PAIRED, n).wait_recv()
            share_slab((x + NX - n - 1) % NX)

    def shared():
        here = next_t.at[matrices(PAIRED)]
        return pltpu.make_async_remote_copy(
            src_ref=here, dst_ref=here, send_sem=pair_send.at[1], recv_sem=pair_recv.at[1],
            device_id=opposite, device_id_type=MESH,
        )

    for head in range(2):
        gradients(head)
    for g in (0, 1, 3):
        reduce_finish(g, 0)
        reduce_start(g, 1)
    pair_finish()
    reduce_start(PAIRED, 0)
    for g in (0, 1):
        reduce_finish(g, 1)
        last_start(g)
    for g in (0, 1):
        renormed(g)
        gather_start(g)
    reduce_finish(3, 1)
    last_start(3)
    reduce_finish(PAIRED, 0)
    reduce_start(PAIRED, 1)
    renormed(3)
    gather_start(3)
    gather_forward(0)
    reduce_finish(PAIRED, 1)
    renormed(PAIRED)
    gather_start(PAIRED)
    for head in range(2):
        exchange(2, q_hbm, q_all, head)
    for g in (1, 3, PAIRED):
        gather_forward(g)
    share()
    loads["query"].wait()

    for head in range(2):
        cols = slice(head * WIDTH, (head + 1) * WIDTH)
        for n in range(3):
            arrived(2, q_all, head, n)
        if head == 0:
            gather_finish(0)
            gather_finish(1)
        else:
            gather_finish(3)
            shared().wait_recv()
        for half in (1, 0):
            rows = slice(half * 2 * ROWS, (half + 1) * 2 * ROWS)
            queries = q_all[rows, cols]
            first = dot(queries, next_t[3 * head], (1, 1))
            second = dot(queries, next_t[3 * head + 1], (1, 1))
            mixed[rows, :] = (first * jax.nn.sigmoid(first) * second).astype(jnp.bfloat16)
            results[rows, cols] = dot(mixed[rows, :], next_t[3 * head + 2], (1, 1)).astype(
                jnp.bfloat16
            )
            for n in ((1, 2) if half else (0,)):
                index = 0 if n == 0 else 1 + core
                send(
                    results.at[slot_rows(1 + n), cols], out_ref.at[:, columns(group, head)],
                    out_send.at[head, n], out_recv.at[head, index], sources[n],
                )
        out_ref[:, columns(group, head)] = results[slot_rows(0), cols]

    for head in range(2):
        for n in range(3):
            there = out_ref.at[:, columns(target_group[n], head)]
            pltpu.make_async_remote_copy(
                src_ref=there, dst_ref=there, send_sem=out_send.at[head, n],
                recv_sem=out_recv.at[head, n], device_id=targets[n], device_id_type=MESH,
            ).wait_recv()
    for copy in started:
        copy.wait_send()
    shared().wait_send()
    for g in range(len(GROUPS)):
        for n in range(len(peers[GROUPS[g][2]])):
            whole_slab(g, n).wait_send()


def finish(staged, next_t, out_ref, gate_ref, down_ref, up_ref, turned, sems):
    copies = [pltpu.make_async_copy(staged, out_ref, sems.at[MATS])]
    copies[0].start()
    same = (
        lax.broadcasted_iota(jnp.int32, (WIDTH, WIDTH), 0)
        == lax.broadcasted_iota(jnp.int32, (WIDTH, WIDTH), 1)
    )
    unit = jnp.where(same, 1.0, 0.0).astype(jnp.bfloat16)
    for m in range(MATS):
        head, kind = divmod(m, 3)
        turned[m] = dot(unit, next_t[m], (1, 1)).astype(jnp.bfloat16)
        copy = pltpu.make_async_copy(
            turned.at[m], (gate_ref, up_ref, down_ref)[kind].at[head], sems.at[m]
        )
        copy.start()
        copies.append(copy)
    for copy in copies:
        copy.wait()


def solution(mesh):
    def step(queries, keys, values, rates, gate_fast, down_fast, up_fast):
        size = {"x": NX, "z": NZ}
        bf16 = jnp.bfloat16

        def per_group(shape):
            return [
                pltpu.VMEM(shape(1 if paired else count, axis), bf16)
                for _, count, axis, paired in GROUPS
            ]

        slab = lambda axis: WIDTH // size[axis]
        rest = lambda axis: NX * NZ // size[axis]
        vmem = pl.BlockSpec(memory_space=pltpu.VMEM)
        anywhere = pl.BlockSpec(memory_space=pltpu.HBM)
        groups = len(GROUPS)
        weight = gate_fast.shape
        outs = (
            jax.ShapeDtypeStruct(queries.shape, bf16),
            jax.ShapeDtypeStruct(weight, bf16),
            jax.ShapeDtypeStruct(weight, bf16),
            jax.ShapeDtypeStruct(weight, bf16),
        )
        staged, next_t = pl.pallas_call(
            kernel,
            out_shape=(
                pltpu.VMEM(queries.shape, bf16),
                pltpu.VMEM((MATS, WIDTH, WIDTH), bf16),
            ),
            in_specs=[anywhere] * 7,
            out_specs=[vmem] * 2,
            scratch_shapes=[
                pltpu.VMEM((ROWS, 8 * WIDTH), bf16),
                pltpu.VMEM((8, ROWS), jnp.float32),
                pltpu.VMEM(weight, bf16),
                pltpu.VMEM(weight, bf16),
                pltpu.VMEM(weight, bf16),
                pltpu.VMEM((ROWS, 8 * WIDTH), bf16),
                pltpu.VMEM((4 * ROWS, PAIR), bf16),
                pltpu.VMEM((4 * ROWS, PAIR), bf16),
                pltpu.VMEM((4 * ROWS, PAIR), bf16),
                pltpu.VMEM((4 * ROWS, WIDTH), bf16),
                pltpu.VMEM((4 * ROWS, WIDTH), bf16),
                pltpu.VMEM((4 * ROWS, WIDTH), bf16),
                pltpu.VMEM((MATS, WIDTH, WIDTH), bf16),
                pltpu.VMEM((4 * ROWS, WIDTH), bf16),
                pltpu.VMEM((4 * ROWS, PAIR), bf16),
                per_group(lambda count, axis: (size[axis] - 1, count, slab(axis), WIDTH)),
                per_group(lambda count, axis: (count, slab(axis), WIDTH)),
                per_group(lambda count, axis: (rest(axis) - 1, count, PIECE, WIDTH)),
                per_group(lambda count, axis: (count, PIECE, WIDTH)),
                per_group(lambda count, axis: (count, PIECE, WIDTH)),
                pltpu.SemaphoreType.DMA((7,)),
                pltpu.SemaphoreType.DMA((3, 2, 3)),
                pltpu.SemaphoreType.DMA((3, 2, 3)),
                pltpu.SemaphoreType.DMA((groups, 2, NZ - 1)),
                pltpu.SemaphoreType.DMA((groups, 2, NZ - 1)),
                pltpu.SemaphoreType.DMA((groups,)),
                pltpu.SemaphoreType.DMA((groups,)),
                pltpu.SemaphoreType.DMA((groups, NZ - 1)),
                pltpu.SemaphoreType.DMA((groups, NZ - 1)),
                pltpu.SemaphoreType.DMA((groups, NZ - 1)),
                pltpu.SemaphoreType.DMA((groups, NZ - 1)),
                pltpu.SemaphoreType.DMA((2, 3)),
                pltpu.SemaphoreType.DMA((2, 3)),
                pltpu.VMEM((WIDTH, WIDTH), bf16),
                pltpu.VMEM((1, WIDTH, WIDTH), bf16),
                pltpu.SemaphoreType.DMA((2,)),
                pltpu.SemaphoreType.DMA((2,)),
            ],
            compiler_params=pltpu.CompilerParams(
                collective_id=0, has_side_effects=True, vmem_limit_bytes=40 << 20
            ),
        )(
            *(
                pltpu.with_memory_space_constraint(array, pltpu.HBM)
                for array in (queries, keys, values, rates.T, gate_fast, down_fast, up_fast)
            )
        )
        return pl.pallas_call(
            finish,
            out_shape=outs,
            in_specs=[vmem] * 2,
            out_specs=[anywhere] * 4,
            scratch_shapes=[
                pltpu.VMEM((MATS, WIDTH, WIDTH), bf16),
                pltpu.SemaphoreType.DMA((MATS + 1,)),
            ],
            compiler_params=pltpu.CompilerParams(vmem_limit_bytes=12 << 20),
        )(staged, next_t)

    tokens = P(("heads", "tokens"), None)
    weights = P("heads", None, None)
    return jax.shard_map(
        step,
        mesh=mesh,
        in_specs=(tokens,) * 4 + (weights,) * 3,
        out_specs=(tokens,) + (weights,) * 3,
        check_vma=False,
    )
```
